512 devices in a mesh: ch: 8 (over x, core), gx: 32 (over z, y_lo), gy: 2 (over y_hi).
Axes of the slice: x: 4, y: 8 (y_hi: 2, y_lo: 4; y = y_hi * 4 + y_lo), z: 8, core: 2. Of those that a mesh axis runs over, the one named last changes fastest.
Arguments:
- features: bfloat16 [128, 16, 2, 1024], P('gx', 'gy', None, 'ch'), may hold values from -6 to 6
- positions: float32 [3, 128, 16, 2], P(None, 'gx', 'gy'), may hold values from 0 to 1
- neighbours: int32 [128, 16, 2, 32], P('gx', 'gy'), may hold values from 0 to 17, as said below
- counts: int32 [128, 16, 2], P('gx', 'gy'), may hold values from 16 to 32
- species: int32 [128, 16, 2], P('gx', 'gy'), may hold values from 0 to 5
- radial_in: float32 [8, 64], replicated, may hold values from -2 to 2
- radial_out: bfloat16 [64, 3, 1024], P(None, None, 'ch'), may hold values from -0.75 to 0.75
- mix_weight: bfloat16 [3, 1024, 1024], P(None, None, 'ch'), may hold values from -0.1875 to 0.1875
- species_weight: float32 [6, 8, 1024], P(None, None, 'ch'), may hold values from -3 to 3
- out_weight: bfloat16 [1024, 1024], P(None, 'ch'), may hold values from -0.1875 to 0.1875
- readout: float32 [1024], P('ch'), may hold values from -0.1875 to 0.1875
Outputs:
- layer_out: bfloat16 [128, 16, 2, 1024], P('gx', 'gy', None, 'ch')
- energy: float32 [128, 16, 2], P('gx', 'gy')
- forces: float32 [3, 128, 16, 2], P(None, 'gx', 'gy')
- feature_grad: bfloat16 [128, 16, 2, 1024], P('gx', 'gy', None, 'ch')
- stress: float32 [3, 3], replicated
The draws below stay inside these ranges and needn't reach their ends.
Inputs may be any that keep to these rules, and one draw needn't show every extreme that they name: `neighbours`: code ((dx + 1) * 3 + dy + 1) * 2 + slot names the atom in that slot of the cell column dx, dy columns away, periodically; never the atom itself.
All inputs are finite; a program needn't handle non-finite values.
Results may differ from the reference program's by a relative error of at most 0.012.
Values may be sent and summed in bfloat16 or wider, within the bound.
No kernel may reach another device: no remote copies, remote signals or barrier semaphores. Data moves between devices by JAX's collectives and lax.ppermute only.
A program may use at most 64 MiB of HBM per device.

```python
import math
import jax
import jax.numpy as jnp
from jax import lax

K = 1024
NBASIS = 8
RHID = 64
NSPEC = 6
NEIGH = 32
SLOTS = 2
NX = 128
NY = 16


def draw_neighbours(key, part):
    key = jax.random.fold_in(key, 11)
    drawn = jax.random.randint(key, (NX, NY, SLOTS, NEIGH), 0, 9 * SLOTS - 1, dtype=jnp.int32)
    own_code = 4 * SLOTS + jnp.arange(SLOTS, dtype=jnp.int32)[None, None, :, None]
    return drawn + (drawn >= own_code).astype(jnp.int32)


def plant(values, own_key, low, top_value):
    place = [jax.random.randint(jax.random.fold_in(own_key, axis), (), 0, length) for axis, length in enumerate(values.shape)]
    longest = values.shape.index(max(values.shape))
    neighbour = place[:longest] + [(place[longest] + 1) % values.shape[longest]] + place[longest + 1:]
    return values.at[tuple(place)].set(low).at[tuple(neighbour)].set(top_value)


def level_of(rng, dims, shards, low, largest):
    loudness, own = 1.0, jax.random.fold_in(rng, 6)
    for axis_at, shards_of in shards:
        heights = jnp.exp(jax.random.uniform(jax.random.fold_in(own, axis_at), (shards_of,), jnp.float32, low / len(shards), largest / len(shards)))
        loudness = loudness * jnp.repeat(heights, dims[axis_at] // shards_of).reshape([-1 if axis == axis_at else 1 for axis in range(len(dims))])
    return loudness


def centred(stream_key, dims, spread, limit, shards=(), kind=jnp.bfloat16):
    values = spread * jax.random.normal(stream_key, dims, jnp.float32)
    if shards:
        values = values * level_of(stream_key, dims, shards, -0.22, 0.18)
    return jnp.clip(values, -limit, limit).astype(kind)


def setup_inputs(seed: int = 0) -> dict:
    streams_of = jax.random.split(jax.random.key(seed), 12)
    return {
        "features": centred(streams_of[0], (NX, NY, SLOTS, K), 1.0, 6.0, ((0, 32), (1, 2), (3, 8))),
        "positions": jnp.clip(1.0 * jax.random.uniform(streams_of[1], (3, NX, NY, SLOTS), jnp.float32) ** level_of(streams_of[1], (3, NX, NY, SLOTS), ((1, 32), (2, 2)), -0.2, 0.2), 0.0, 1.0),
        "neighbours": draw_neighbours(jax.random.fold_in(streams_of[11], 71), 0),
        "counts": plant(jax.random.randint(streams_of[3], (NX, NY, SLOTS), NEIGH // 2, NEIGH + 1), jax.random.fold_in(streams_of[3], 1), NEIGH // 2, NEIGH).astype(jnp.int32),
        "species": plant(jax.random.randint(streams_of[4], (NX, NY, SLOTS), 0, NSPEC), jax.random.fold_in(streams_of[4], 1), 0, NSPEC - 1).astype(jnp.int32),
        "radial_in": centred(streams_of[5], (NBASIS, RHID), NBASIS ** -0.5, 2.0, (), jnp.float32),
        "radial_out": centred(streams_of[6], (RHID, 3, K), RHID ** -0.5, 0.75, ((2, 8),)),
        "mix_weight": centred(streams_of[7], (3, K, K), K ** -0.5, 0.1875, ((2, 8),)),
        "species_weight": centred(streams_of[8], (NSPEC, 8, K), 0.5, 3.0, ((2, 8),), jnp.float32),
        "out_weight": centred(streams_of[9], (K, K), K ** -0.5, 0.1875, ((1, 8),)),
        "readout": centred(streams_of[10], (K,), K ** -0.5, 0.1875, ((0, 8),), jnp.float32),
    }


cutoff = 3.2
message_scale = 0.25
degree_bounds = ((0, 1), (1, 4), (4, 9))

def geometry(offsets, radial_in):
    squared = lax.optimization_barrier(jnp.sum(offsets * offsets, axis=0)) + 0.25
    distance = jnp.sqrt(squared)
    unit_x = offsets[0] / distance
    unit_y = offsets[1] / distance
    unit_z = offsets[2] / distance
    harmonic = jnp.stack([jnp.ones_like(unit_x), unit_x, unit_y, unit_z, unit_x * unit_y, unit_y * unit_z, 1.5 * unit_z * unit_z - 0.5, unit_x * unit_z, 0.5 * (unit_x * unit_x - unit_y * unit_y)])
    ratio = distance / cutoff
    envelope = (1.0 - ratio * ratio) ** 2
    orders = jnp.arange(1, radial_in.shape[0] + 1).astype(jnp.float32)
    basis = jnp.sin(math.pi * orders[:, None] * ratio[None, :]) * (envelope / distance)[None, :]
    hidden = jax.nn.silu(jnp.einsum('be,bh->eh', basis, radial_in, precision=lax.Precision.HIGHEST))
    return (harmonic, hidden)

def contract(mixed, chosen):
    center = mixed[:, 0]
    vec_x = mixed[:, 1]
    vec_y = mixed[:, 2]
    vec_z = mixed[:, 3]
    quad_a = mixed[:, 4]
    quad_b = mixed[:, 5]
    quad_c = mixed[:, 6]
    quad_d = mixed[:, 7]
    quad_e = mixed[:, 8]
    vec_sq = vec_x * vec_x + vec_y * vec_y + vec_z * vec_z
    quad_sq = quad_a * quad_a + quad_b * quad_b + quad_c * quad_c + quad_d * quad_d + quad_e * quad_e
    cubic = (quad_e - quad_c) * vec_x * vec_x - (quad_e + quad_c) * vec_y * vec_y + 2.0 * quad_c * vec_z * vec_z + 2.0 * (quad_a * vec_x * vec_y + quad_b * vec_y * vec_z + quad_d * vec_x * vec_z)
    terms = jnp.stack([center, center * center, vec_sq, quad_sq, center * center * center, center * vec_sq, center * quad_sq, cubic], axis=1)
    return lax.optimization_barrier(jnp.sum(terms * chosen, axis=1))

def reference(features, positions, neighbours, counts, species, radial_in, radial_out, mix_weight, species_weight, out_weight, readout):
    rows_x, rows_y, slot_count, chan_total = features.shape
    neigh_count = neighbours.shape[-1]
    per_block = rows_y * slot_count
    atom_count = rows_x * per_block
    pos_all = positions.reshape(3, atom_count)
    feat_all = features.reshape(atom_count, chan_total)

    def edges_of(row):
        codes = lax.dynamic_index_in_dim(neighbours, row, 0, keepdims=False).reshape(per_block, neigh_count)
        step_x = codes // (3 * slot_count) - 1
        step_y = codes // slot_count % 3 - 1
        slot_nb = codes % slot_count
        local = jnp.arange(per_block, dtype=jnp.int32)
        cell_y = (local // slot_count)[:, None]
        target = (((row + step_x) % rows_x * rows_y + (cell_y + step_y) % rows_y) * slot_count + slot_nb).astype(jnp.int32)
        own_index = (row * per_block + local).astype(jnp.int32)
        pos_nb = pos_all[:, target.reshape(-1)].reshape(3, per_block, neigh_count)
        pos_own = pos_all[:, own_index]
        offsets = jnp.stack([step_x.astype(jnp.float32) + pos_nb[0] - pos_own[0][:, None], step_y.astype(jnp.float32) + pos_nb[1] - pos_own[1][:, None], pos_nb[2] - pos_own[2][:, None]]).reshape(3, per_block * neigh_count)
        live_count = lax.dynamic_index_in_dim(counts, row, 0, keepdims=False).reshape(per_block, 1)
        live = (jnp.arange(neigh_count, dtype=jnp.int32)[None, :] < live_count).astype(jnp.float32)
        return (target, own_index, offsets, live)

    def radial_parts(offsets, live, target):
        harmonic, hidden = geometry(offsets, radial_in)
        harm_live = (harmonic.reshape(9, per_block, neigh_count) * live[None]).transpose(1, 2, 0)
        hidden_bf = hidden.astype(jnp.bfloat16)
        nb_feat = feat_all[target.reshape(-1)].reshape(per_block, neigh_count, chan_total)
        radials = []
        for degree in range(3):
            radial = jnp.dot(hidden_bf, radial_out[:, degree, :], preferred_element_type=jnp.float32)
            radials.append(radial.reshape(per_block, neigh_count, chan_total))
        return (harm_live, nb_feat, radials)

    def forward_block(row):
        target, own_index, offsets, live = edges_of(row)
        harm_live, nb_feat, radials = radial_parts(offsets, live, target)
        parts = []
        for degree, (first, last) in enumerate(degree_bounds):
            product = radials[degree] * nb_feat.astype(jnp.float32)
            parts.append(message_scale * jnp.einsum('anm,ank->amk', harm_live[:, :, first:last], product, precision=lax.Precision.HIGHEST))
        return jnp.concatenate(parts, axis=1).astype(jnp.bfloat16)
    block_rows = jnp.arange(rows_x, dtype=jnp.int32)
    message = lax.map(forward_block, block_rows).reshape(atom_count, 9, chan_total)
    mixed_parts = []
    for degree, (first, last) in enumerate(degree_bounds):
        block = message[:, first:last, :].reshape(-1, chan_total)
        mixed_parts.append(jnp.dot(block, mix_weight[degree], preferred_element_type=jnp.float32).reshape(atom_count, last - first, chan_total))
    mixed = jnp.concatenate(mixed_parts, axis=1)
    onehot = (species.reshape(atom_count, 1) == jnp.arange(species_weight.shape[0], dtype=jnp.int32)[None, :]).astype(jnp.float32)
    chosen = jnp.einsum('as,stk->atk', onehot, species_weight, precision=lax.Precision.HIGHEST)
    products = contract(mixed, chosen).astype(jnp.bfloat16)
    layer = jnp.dot(products, out_weight, preferred_element_type=jnp.float32) + feat_all.astype(jnp.float32)
    energy = lax.optimization_barrier(jnp.sum(layer * readout[None, :], axis=1))
    vector = jnp.dot(out_weight.astype(jnp.float32), readout, precision=lax.Precision.HIGHEST)
    cotangent = jnp.broadcast_to(vector[None, :], (atom_count, chan_total))
    dummy, pullback = jax.vjp(lambda values: contract(values, chosen), mixed)
    adjoint_bf = pullback(cotangent)[0].astype(jnp.bfloat16)
    adjoint_parts = []
    for degree, (first, last) in enumerate(degree_bounds):
        block = adjoint_bf[:, first:last, :].reshape(-1, chan_total)
        adjoint_parts.append(jnp.dot(block, mix_weight[degree].T, preferred_element_type=jnp.float32).reshape(atom_count, last - first, chan_total))
    adjoint_message = jnp.concatenate(adjoint_parts, axis=1)

    def back_step(carry, row):
        grad_feat, grad_force, virial = carry
        target, own_index, offsets, live = edges_of(row)
        harm_live, nb_feat, radials = radial_parts(offsets, live, target)
        dummy_out, geo_back = jax.vjp(lambda values: geometry(values, radial_in), offsets)
        adjoint_rows = lax.dynamic_slice_in_dim(adjoint_message, row * per_block, per_block, 0)
        nb_float = nb_feat.astype(jnp.float32)
        harm_grads = []
        feature_back = jnp.zeros((per_block, neigh_count, chan_total), jnp.float32)
        grad_hidden = jnp.zeros((per_block * neigh_count, radial_out.shape[0]), jnp.float32)
        for degree, (first, last) in enumerate(degree_bounds):
            grad_slice = adjoint_rows[:, first:last, :]
            grad_prod = message_scale * jnp.einsum('anm,amk->ank', harm_live[:, :, first:last], grad_slice, precision=lax.Precision.HIGHEST)
            product = radials[degree] * nb_float
            harm_grads.append(message_scale * jnp.einsum('amk,ank->anm', grad_slice, product, precision=lax.Precision.HIGHEST))
            grad_radial = (grad_prod * nb_float).reshape(-1, chan_total).astype(jnp.bfloat16)
            feature_back = feature_back + grad_prod * radials[degree]
            grad_hidden = grad_hidden + lax.dot_general(grad_radial, radial_out[:, degree, :], (((1,), (1,)), ((), ())), preferred_element_type=jnp.float32)
        harm_grad = (jnp.concatenate(harm_grads, axis=2) * live[:, :, None]).transpose(2, 0, 1).reshape(9, -1)
        edge_grad = geo_back((harm_grad, grad_hidden))[0]
        own_sum = lax.optimization_barrier(jnp.sum(edge_grad.reshape(3, per_block, neigh_count), axis=2))
        grad_force = grad_force.at[:, own_index].add(own_sum)
        grad_force = grad_force.at[:, target.reshape(-1)].add(-edge_grad)
        grad_feat = grad_feat.at[target.reshape(-1)].add(feature_back.reshape(-1, chan_total))
        virial = virial + jnp.einsum('ae,be->ab', offsets, edge_grad, precision=lax.Precision.HIGHEST)
        return ((grad_feat, grad_force, virial), None)
    start = (jnp.zeros((atom_count, chan_total), jnp.float32), jnp.zeros((3, atom_count), jnp.float32), jnp.zeros((3, 3), jnp.float32))
    (grad_feat, grad_force, virial), dummy_rest = lax.scan(back_step, start, block_rows)
    layer_out = layer.astype(jnp.bfloat16).reshape(rows_x, rows_y, slot_count, chan_total)
    feature_grad = (grad_feat + readout[None, :]).astype(jnp.bfloat16).reshape(rows_x, rows_y, slot_count, chan_total)
    return (layer_out, energy.reshape(rows_x, rows_y, slot_count), grad_force.reshape(3, rows_x, rows_y, slot_count), feature_grad, virial / atom_count)
```

```python
import functools
import math

import jax
import jax.numpy as jnp
from jax import lax
from jax.experimental import pallas as pl
from jax.experimental.pallas import tpu as pltpu
from jax.sharding import Mesh, PartitionSpec as P

f32 = jnp.float32
bf16 = jnp.bfloat16
cutoff = 3.2
message_scale = 0.25
degree_bounds = ((0, 1), (1, 4), (4, 9))
HIGHEST = lax.Precision.HIGHEST

ATOMS = 32
NEIGH = 32
EDGES = ATOMS * NEIGH
GROUP = 1024
GROUPS = EDGES // GROUP
PER = GROUP // NEIGH
CH = 128
WIDE = 256
HID = 64
MSG = 9 * ATOMS
PAY = MSG + 16
BACK = MSG + ATOMS
SENT = BACK + 16

VMEM_LIMIT = 48 * 1024 * 1024


def nn(a, b):
    return lax.dot_general(a, b, (((1,), (0,)), ((), ())), preferred_element_type=f32)


def nt(a, b):
    return lax.dot_general(a, b, (((1,), (1,)), ((), ())), preferred_element_type=f32)


def tn(a, b):
    return lax.dot_general(a, b, (((0,), (0,)), ((), ())), preferred_element_type=f32)


def split3(v):
    hi = v.astype(bf16)
    rest = v - hi.astype(f32)
    mid = rest.astype(bf16)
    low = (rest - mid.astype(f32)).astype(bf16)
    return hi, mid, low


def split2(v):
    hi = v.astype(bf16)
    return hi, (v - hi.astype(f32)).astype(bf16)


def stacked(parts):
    return jnp.concatenate([part.astype(f32) for part in parts], axis=0)


def iota(shape, dim):
    return lax.broadcasted_iota(jnp.int32, shape, dim)


def call(kernel, out_shape, scratch=(), us=1.0):
    def run(scalars, *arrays):
        return pl.pallas_call(
            kernel,
            out_shape=out_shape,
            in_specs=[pl.BlockSpec(memory_space=pltpu.SMEM)]
            + [pl.BlockSpec(memory_space=pltpu.VMEM)] * len(arrays),
            out_specs=jax.tree.map(lambda _: pl.BlockSpec(memory_space=pltpu.VMEM), out_shape),
            scratch_shapes=list(scratch),
            cost_estimate=pl.CostEstimate(
                flops=int(us * 1e9), bytes_accessed=1 << 18, transcendentals=0
            ),
            compiler_params=pltpu.CompilerParams(vmem_limit_bytes=VMEM_LIMIT),
        )(scalars, *arrays)

    return run


SP_SPEC = 3 * HID
SP_READ = SP_SPEC + 144
SP_OUT = SP_READ + 16
SP_MIX = SP_OUT + 1024
SP_ROWS = SP_MIX + 3 * 1024


def send_kernel(sc, feat, pos, send):
    tiles = [pos[d, r] for d in range(3) for r in range(4)]
    pick = jnp.where(((iota((8, CH), 1) >> 1) & 7) == iota((8, CH), 0), 1.0, 0.0)
    spread = lax.dot_general(
        jnp.concatenate(tiles, axis=0),
        pick,
        (((1,), (0,)), ((), ())),
        precision=HIGHEST,
        preferred_element_type=f32,
    )
    r8 = iota((8, CH), 0)
    l8 = iota((8, CH), 1)
    here = (l8 < 64) & ((l8 >> 4) == (r8 >> 1)) & ((l8 & 1) == (r8 & 1))
    lines = [
        jnp.sum(jnp.where(here, spread[8 * d : 8 * d + 8], 0.0), axis=0, keepdims=True)
        for d in range(3)
    ]
    row = iota((16, CH), 0)
    rows = jnp.zeros((16, CH), f32)
    for d in range(3):
        for k, part in enumerate(split3(lines[d])):
            rows = jnp.where(row == 3 * k + d, part.astype(f32), rows)
    for c in range(2):
        moved = (rows if c == 0 else pltpu.roll(rows, CH - 16, 1)).astype(bf16)
        for y in range(2):
            send[2 * c + y, 0:48] = feat[16 * c : 16 * c + 48]
            send[2 * c + y, 48:64] = moved


def pack_kernel(sc, rad_out, spec, read, ow, mw, spack):
    spack[SP_OUT:SP_MIX] = ow[...]
    spack[SP_MIX:SP_ROWS] = mw[...]
    spack[0:SP_SPEC] = rad_out[...]
    parts = split3(spec[...])
    for k in range(3):
        spack[SP_SPEC + 48 * k : SP_SPEC + 48 * (k + 1)] = parts[k]
    r0, r1, r2 = split3(read[...])
    rr = iota((16, CH), 0)
    rows = (
        jnp.where(rr == 0, r0.astype(f32), 0.0)
        + jnp.where(rr == 1, r1.astype(f32), 0.0)
        + jnp.where(rr == 2, r2.astype(f32), 0.0)
    )
    spack[SP_READ:SP_OUT] = rows.astype(bf16)


def edge_kernel(sc, recv, out):
    start = pl.multiple_of(32 * sc[0], 16)
    for s in range(4):
        out[s, 0:16] = recv[s, pl.ds(start, 16)]
        out[s, 16:32] = recv[s, 48:64]


def feat_table(recv, xrow, yh):
    halves = []
    for cs in range(2):
        o = 2 * cs + yh
        t = 2 * cs + 1 - yh
        halves.append(
            jnp.concatenate([recv[o, 0:48], recv[t, 0:48], xrow[o, 0:16], xrow[t, 0:16]], axis=0)
        )
    return jnp.concatenate(halves, axis=1)


def pos_table(recv, xrow, c, yh):
    lane = iota((16, CH), 1)

    def turned(value, to):
        first = pltpu.roll(value, to - 32, 1)
        return jnp.where(c == 0, first, pltpu.roll(value, to, 1))

    own = recv[yh, 48:64].astype(f32)
    across = pltpu.roll(recv[1 - yh, 48:64].astype(f32), 48, 1)
    row_own = turned(xrow[yh, 16:32].astype(f32), 96)
    row_across = turned(xrow[1 - yh, 16:32].astype(f32), 112)
    table = jnp.where(
        lane < 48, own, jnp.where(lane < 96, across, jnp.where(lane < 112, row_own, row_across))
    )
    return table.astype(bf16)


def ordered(c, own, other):
    first = jnp.where(c == 0, own, other)
    second = jnp.where(c == 0, other, own)
    return first, second


def own_index(c, start, count):
    atom = (iota((1, count), 1) >> 5) + start
    return ((atom >> 4) + c) * 16 + (atom & 15)


def prep_kernel(sc, meta, spk_o, spk_p, rows_ref, rad_ref, rad_t_ref, vec_ref, cho_ref, tmp):
    c = sc[0]
    start = pl.multiple_of(c * ATOMS, ATOMS)
    mine = meta[pl.ds(start, ATOMS), :]
    codes = mine[:, 0:NEIGH].astype(f32).astype(bf16)
    spread = (iota((NEIGH, EDGES), 0) == (iota((NEIGH, EDGES), 1) & 31)).astype(bf16)
    at_atom = iota((ATOMS, EDGES), 0) == (iota((ATOMS, EDGES), 1) >> 5)
    code = jnp.sum(jnp.where(at_atom, nn(codes, spread), 0.0), axis=0, keepdims=True)
    code = code.astype(jnp.int32)
    counts = mine[:, NEIGH : NEIGH + 1].astype(f32)
    count = jnp.sum(jnp.where(at_atom, counts, 0.0), axis=0, keepdims=True)
    lane = iota((1, EDGES), 1)
    slot = lane & 31
    atom = lane >> 5
    col = (atom >> 1) & 7
    third = (code * 43) >> 8
    step_x = third - 1
    step_y = (code >> 1) - 3 * third - 1
    q = (atom >> 4) + step_x + c
    y = col + step_y
    across = jnp.where((y < 0) | (y > 7), 1, 0)
    inside = (q >= 0) & (q <= 2)
    idx = (
        jnp.where(inside, across * 48 + q * 16, 96 + across * 16) + (y & 7) * 2 + (code & 1)
    )
    rows_ref[0:1] = idx.astype(f32)
    rows_ref[1:2] = jnp.where(slot.astype(f32) < count, message_scale, 0.0)
    rows_ref[2:3] = step_x.astype(f32)
    rows_ref[3:4] = step_y.astype(f32)
    rows_ref[4:8] = jnp.zeros((4, EDGES), f32)
    for degree in range(3):
        rows = slice(degree * HID, (degree + 1) * HID)
        first, second = ordered(c, spk_o[rows].astype(f32), spk_p[rows].astype(f32))
        wide = jnp.concatenate([first, second], axis=1)
        rad_ref[degree] = wide.astype(bf16)
        rad_t_ref[degree] = wide.T.astype(bf16)
    vec = 0.0
    for ref in (spk_o, spk_p):
        vec = vec + nt(ref[SP_READ:SP_OUT], ref[SP_OUT:SP_MIX])
    vec = vec[0:1] + vec[1:2] + vec[2:3]
    tmp[...] = jnp.zeros((16, WIDE), f32)
    for b in range(4):
        parts = split3(vec[:, b * WIDE : (b + 1) * WIDE])
        for k in range(3):
            tmp[3 * b + k : 3 * b + k + 1] = parts[k].astype(f32)
    vec_ref[...] = tmp[...].astype(bf16)
    species = mine[:, NEIGH + 1 : NEIGH + 2]
    whole = []
    for ref in (spk_o, spk_p):
        whole.append(
            sum(ref[SP_SPEC + 48 * k : SP_SPEC + 48 * (k + 1)].astype(f32) for k in (2, 1, 0))
        )
    spec = jnp.concatenate(whole, axis=1)
    for t in range(8):
        value = jnp.zeros((ATOMS, WIDE), f32)
        for s in range(6):
            value = jnp.where(species == s, spec[8 * s + t : 8 * s + t + 1], value)
        cho_ref[t] = value


def forward_kernel(
    sc, recv, xrow, prep, rad_in, rad_t, vec, pay, geo, hid_ref, slope, hot_ref, feat_ref, acc
):
    c = sc[0]
    yh = sc[1]
    idx = prep[0:1].astype(jnp.int32)
    scaled = prep[1:2]
    rows = iota((128, EDGES), 0)
    hot = jnp.where(rows == idx, 1.0, 0.0)
    diff = (hot - jnp.where(rows == own_index(c, 0, EDGES), 1.0, 0.0)).astype(bf16)
    moved = nn(pos_table(recv, xrow, c, yh), diff)
    rel = moved[0:3] + moved[3:6] + moved[6:9]
    rx = prep[2:3] + rel[0:1]
    ry = prep[3:4] + rel[1:2]
    rz = rel[2:3]
    rho = jnp.sqrt(rx * rx + ry * ry + rz * rz + 0.25)
    inv = 1.0 / rho
    ux, uy, uz = rx * inv, ry * inv, rz * inv
    ratio = rho / cutoff
    theta = math.pi * ratio
    gap = 1.0 - ratio * ratio
    env = gap * gap * inv
    turns = (iota((8, 1), 0) + 1).astype(f32) * theta
    sins = jnp.sin(turns)
    geo[0:1] = idx.astype(f32)
    geo[1:2] = scaled
    geo[2:3] = rx
    geo[3:4] = ry
    geo[4:5] = rz
    geo[5:6] = rho
    geo[6:7] = inv
    geo[7:8] = env
    geo[8:16] = sins
    geo[16:24] = jnp.cos(turns)
    basis = sins * env
    r_hi, r_mid, r_lo = split3(rad_in[...])
    b_hi, b_mid, b_lo = split3(basis)
    z = tn(
        stacked((r_hi, r_hi, r_mid, r_hi, r_lo, r_mid)).astype(bf16),
        stacked((b_hi, b_mid, b_hi, b_lo, b_hi, b_mid)).astype(bf16),
    )
    sig = lax.logistic(z)
    hidden = (z * sig).astype(bf16)
    hid_ref[...] = hidden
    slope[...] = sig * (1.0 + z * (1.0 - sig))
    harm = (
        scaled,
        scaled * ux,
        scaled * uy,
        scaled * uz,
        scaled * ux * uy,
        scaled * uy * uz,
        scaled * (1.5 * uz * uz - 0.5),
        scaled * ux * uz,
        scaled * 0.5 * (ux * ux - uy * uy),
    )
    for m in range(9):
        geo[24 + m : 25 + m] = harm[m]
    feat_t = feat_table(recv, xrow, yh).astype(f32).T.astype(bf16)
    block = iota((PER, GROUP), 0) == (iota((PER, GROUP), 1) >> 5)
    hot_b = hot.astype(bf16)
    hot_ref[...] = hot_b
    feat_ref[...] = feat_t
    for g in range(GROUPS):
        at = slice(g * GROUP, (g + 1) * GROUP)
        nb = nn(feat_t, hot_b[:, at])
        hid = hidden[:, at]
        radials = nn(rad_t[...].reshape(3 * WIDE, HID), hid)
        for degree, (first, last) in enumerate(degree_bounds):
            p_hi, p_lo = split2(radials[degree * WIDE : (degree + 1) * WIDE] * nb)
            blocks = [jnp.where(block, harm[m][:, at], 0.0) for m in range(first, last)]
            y_hi, y_lo = split2(jnp.concatenate(blocks, axis=0))
            both = nt(jnp.concatenate([y_hi, y_lo], axis=0), p_hi)
            half = (last - first) * PER
            msg = both[:half] + both[half:] + nt(y_hi, p_lo)
            for k in range(last - first):
                r0 = (first + k) * ATOMS + g * PER
                acc[r0 : r0 + PER] = msg[k * PER : (k + 1) * PER]
    pay[0:MSG] = acc[0:MSG].astype(bf16)
    pay[MSG:PAY] = vec[...]


TOP = 14.0


def level_of(value):
    peak = jnp.max(jnp.max(jnp.abs(value), axis=0, keepdims=True), axis=1, keepdims=True)
    return jnp.clip(jnp.floor(jnp.log2(jnp.maximum(peak, 1e-30))), -100.0, 100.0)


def scale_of(adjp, s, row):
    return jnp.exp2(adjp[s, BACK + row : BACK + row + 1, 0:1] - TOP)


def mix_of(spk_o, spk_p, degree):
    at = slice(SP_MIX + 1024 * degree, SP_MIX + 1024 * (degree + 1))
    return jnp.concatenate([spk_o[at], spk_p[at]], axis=1)


def mix_kernel(sc, full, spk_o, spk_p, cho, out):
    c = sc[0]
    x = sc[2]
    at = (iota((16, WIDE), 0) * 43) >> 7
    tall = jnp.zeros((16, WIDE), f32)
    for s in range(4):
        tall = tall + full[s, MSG:PAY, :].astype(f32)
    vec = jnp.sum(jnp.where(at == x, tall, 0.0), axis=0, keepdims=True)
    vec_o, vec_p = ordered(c, vec[:, 0:CH], vec[:, CH:WIDE])
    vec = jnp.concatenate([vec_o, vec_p], axis=1)
    mixed = []
    for degree, (first, last) in enumerate(degree_bounds):
        rows = slice(first * ATOMS, last * ATOMS)
        lhs = jnp.concatenate([full[s, rows, :] for s in range(4)], axis=1)
        both = nn(lhs, mix_of(spk_o, spk_p, degree))
        for m in range(last - first):
            mixed.append(both[m * ATOMS : (m + 1) * ATOMS])

    chosen = [cho[t] for t in range(8)]
    cen, ax, ay, az, qa, qb, qc, qd, qe = mixed
    vec_sq = ax * ax + ay * ay + az * az
    quad_sq = qa * qa + qb * qb + qc * qc + qd * qd + qe * qe
    up = qe - qc
    down = qe + qc
    cubic = (
        up * ax * ax
        - down * ay * ay
        + 2.0 * qc * az * az
        + 2.0 * (qa * ax * ay + qb * ay * az + qd * ax * az)
    )
    cen_sq = cen * cen
    products = (
        cen * chosen[0]
        + cen_sq * chosen[1]
        + vec_sq * chosen[2]
        + quad_sq * chosen[3]
        + cen_sq * cen * chosen[4]
        + cen * vec_sq * chosen[5]
        + cen * quad_sq * chosen[6]
        + cubic * chosen[7]
    )
    first, second = ordered(c, products[:, 0:CH], products[:, CH:WIDE])
    prod = jnp.concatenate([first, second], axis=1).astype(bf16).astype(f32)
    w = [vec * value for value in chosen]
    a_scale = 2.0 * (w[2] + cen * w[5])
    q_scale = 2.0 * (w[3] + cen * w[6])
    w7 = w[7]
    tw7 = 2.0 * w7
    grads = [
        w[0] + 2.0 * cen * w[1] + 3.0 * cen_sq * w[4] + vec_sq * w[5] + quad_sq * w[6],
        a_scale * ax + tw7 * (up * ax + qa * ay + qd * az),
        a_scale * ay + tw7 * (qa * ax - down * ay + qb * az),
        a_scale * az + tw7 * (2.0 * qc * az + qb * ay + qd * ax),
        q_scale * qa + tw7 * ax * ay,
        q_scale * qb + tw7 * ay * az,
        q_scale * qc + w7 * (2.0 * az * az - ax * ax - ay * ay),
        q_scale * qd + tw7 * ax * az,
        q_scale * qe + w7 * (ax * ax - ay * ay),
    ]
    backs = []
    for degree, (first, last) in enumerate(degree_bounds):
        adj = jnp.concatenate(grads[first:last], axis=0).astype(bf16)
        backs.append(nt(adj, mix_of(spk_o, spk_p, degree)))
    back = jnp.concatenate(backs, axis=0)
    level_back, level_prod = level_of(back), level_of(prod)
    back = back * jnp.exp2(TOP - level_back)
    prod = prod * jnp.exp2(TOP - level_prod)
    row = iota((16, WIDE), 0)
    levels = jnp.where(row == 0, level_back, jnp.where(row == 1, level_prod, 0.0))
    for s in range(4):
        out[s, 0:MSG, :] = back[:, s * WIDE : (s + 1) * WIDE]
        out[s, MSG:BACK, :] = prod
        out[s, BACK:SENT, :] = levels


def backward_kernel(
    sc, hot, feat_t, geo, hidden, slope, rad, rad_t, rad_in, adjp, to_y, main, out
):
    c = sc[0]
    yh = sc[1]
    adjm = adjp[0, 0:MSG, :] * scale_of(adjp, 0, 0)
    for s in range(1, 4):
        adjm = adjm + adjp[s, 0:MSG, :] * scale_of(adjp, s, 0)
    r_hi, r_lo = split2(rad_in[...])
    outer = jnp.concatenate([r_hi, r_hi, r_lo], axis=1)
    order = (iota((8, 1), 0) + 1).astype(f32)
    r8 = iota((8, GROUP), 0)
    rows = iota((128, GROUP), 0)
    block = iota((PER, GROUP), 0) == (iota((PER, GROUP), 1) >> 5)

    def rows_of(x, y, z):
        return jnp.where(r8 == 0, x, jnp.where(r8 == 1, y, jnp.where(r8 == 2, z, 0.0)))

    feats = jnp.zeros((128, WIDE), f32)
    found = jnp.zeros((24, CH + 32), f32)
    for g in range(GROUPS):
        at = slice(g * GROUP, (g + 1) * GROUP)
        hot_g = hot[:, at]
        nb = nn(feat_t[...], hot_g)
        hid = hidden[:, at]
        radials = nn(rad_t[...].reshape(3 * WIDE, HID), hid)
        gh = jnp.zeros((HID, GROUP), f32)
        fb = jnp.zeros((WIDE, GROUP), f32)
        gys = []
        scaled = geo[1:2, at]
        for degree, (first, last) in enumerate(degree_bounds):
            radial = radials[degree * WIDE : (degree + 1) * WIDE]
            prod = (radial * nb).astype(bf16)
            blocks = [jnp.where(block, geo[24 + m : 25 + m, at], 0.0) for m in range(first, last)]
            y_hi, y_lo = split2(jnp.concatenate(blocks, axis=0))
            pieces = [
                adjm[m * ATOMS + g * PER : m * ATOMS + (g + 1) * PER] for m in range(first, last)
            ]
            a_hi, a_lo = split2(jnp.concatenate(pieces, axis=0))
            grad_prod = tn(
                jnp.concatenate([a_hi, a_lo, a_hi], axis=0),
                jnp.concatenate([y_hi, y_hi, y_lo], axis=0),
            )
            both = nn(jnp.concatenate([a_hi, a_lo], axis=0), prod)
            half = (last - first) * PER
            over = both[:half] + both[half:]
            for k in range(last - first):
                part = jnp.where(block, over[k * PER : (k + 1) * PER], 0.0)
                gys.append(scaled * jnp.sum(part, axis=0, keepdims=True))
            gh = gh + nn(rad[degree], (grad_prod * nb).astype(bf16))
            fb = fb + grad_prod * radial
        feats = feats + nt(hot_g, fb.astype(bf16))
        rx, ry, rz = geo[2:3, at], geo[3:4, at], geo[4:5, at]
        rho, inv, env = geo[5:6, at], geo[6:7, at], geo[7:8, at]
        d_hi, d_lo = split2(gh * slope[:, at])
        dbasis = nn(outer, jnp.concatenate([d_hi, d_lo, d_hi], axis=0))
        ratio = rho / cutoff
        gap = 1.0 - ratio * ratio
        by_cos = jnp.sum(dbasis * order * geo[16:24, at], axis=0, keepdims=True)
        by_sin = jnp.sum(dbasis * geo[8:16, at], axis=0, keepdims=True)
        drho = by_cos * (math.pi / cutoff) * env - by_sin * inv * (
            env + (4.0 / cutoff) * ratio * gap
        )
        ux, uy, uz = rx * inv, ry * inv, rz * inv
        gx_ = gys[1] + gys[4] * uy + gys[7] * uz + gys[8] * ux
        gy_ = gys[2] + gys[4] * ux + gys[5] * uz - gys[8] * uy
        gz_ = gys[3] + gys[5] * uy + 3.0 * gys[6] * uz + gys[7] * ux
        along = drho - (gx_ * ux + gy_ * uy + gz_ * uz) * inv
        eg = rows_of(gx_ * inv + ux * along, gy_ * inv + uy * along, gz_ * inv + uz * along)
        diff = jnp.where(rows == own_index(c, g * PER, GROUP), 1.0, 0.0) - hot_g.astype(f32)
        places = stacked(split3(rows_of(rx, ry, rz)) + (jnp.zeros((8, GROUP), f32),))
        against = jnp.concatenate([diff, places], axis=0).astype(bf16)
        found = found + nt(stacked(split3(eg)).astype(bf16), against)
    main[0:48] = feats[0:48]
    main[48:64] = feats[96:112]
    to_y[0:48] = feats[48:96].astype(bf16)
    to_y[48:64] = feats[112:128].astype(bf16)
    found = found[0:8] + found[8:16] + found[16:24]
    force = found[:, 0:CH]
    lane = iota((1, CH), 1)
    cross = jnp.concatenate([found[:, CH : CH + 32], jnp.zeros((8, CH - 32), f32)], axis=1)
    cross = cross + pltpu.roll(cross, CH - 8, 1) + pltpu.roll(cross, CH - 16, 1)
    virial = jnp.zeros((1, CH), f32)
    for a in range(3):
        for b in range(3):
            to = 64 + 3 * a + b
            virial = jnp.where(lane == to, pltpu.roll(cross, to - a, 1)[b : b + 1], virial)

    def placed(first, count, to):
        moved = force if to == first else pltpu.roll(force, (to - first) % CH, 1)
        return jnp.where((lane >= to) & (lane < to + count), moved, 0.0)

    def by_core(first, count, to_0, to_1):
        return jnp.where(c == 0, placed(first, count, to_0), placed(first, count, to_1))

    own, beside = sc[3], sc[4]
    goals = (
        (2 * own + yh, by_core(0, 48, 0, 16)),
        (2 * own + 1 - yh, by_core(48, 48, 0, 16)),
        (2 * beside + yh, by_core(96, 16, 48, 0)),
        (2 * beside + 1 - yh, by_core(112, 16, 48, 0)),
    )
    row = iota(out.shape, 0)
    odd = (row & 1) == 1
    total = jnp.where(odd, virial, 0.0)
    for device, value in goals:
        upper = value[0:1] + pltpu.roll(value, 64, 1)[1:2]
        chunk = jnp.where(odd, value[2:3], upper)
        total = total + jnp.where((row >> 1) == device, chunk, 0.0)
    out[...] = total


def layer_kernel(sc, recv, adjp, spk_o, spk_p, layer_ref, level_ref):
    c = sc[0]
    yh = sc[1]
    weights = jnp.concatenate([spk_o[SP_OUT:SP_MIX], spk_p[SP_OUT:SP_MIX]], axis=1)
    parts = [adjp[s, MSG:BACK, :] * scale_of(adjp, s, 1) for s in range(4)]
    both = nn(jnp.concatenate(parts, axis=1).astype(bf16), weights)
    first, second = ordered(c, both[:, 0:CH], both[:, CH:WIDE])
    start = pl.multiple_of(c * 16, 16)
    own_feat = jnp.concatenate(
        [recv[2 * cs + yh, pl.ds(start, ATOMS), :].astype(f32) for cs in range(2)], axis=1
    )
    layer = jnp.concatenate([first, second], axis=1) + own_feat
    layer_ref[...] = layer.astype(bf16)
    ra, rb = ordered(
        c, spk_o[SP_READ:SP_OUT].astype(f32), spk_p[SP_READ:SP_OUT].astype(f32)
    )
    read = jnp.concatenate([ra, rb], axis=1)
    read = read[0:1] + read[1:2] + read[2:3]
    energy = jnp.sum(layer * read, axis=1, keepdims=True)
    lane = iota((ATOMS, CH), 1)
    row = iota((ATOMS, CH), 0)
    level = jnp.sum(jnp.where(lane == row + ATOMS * c, energy, 0.0), axis=0, keepdims=True)
    level_ref[...] = jnp.broadcast_to(level, (8, CH))


def merge_kernel(sc, main, from_y, xback, layer, stay, to_core, acc):
    c = sc[0]
    acc[...] = main[0:48] + from_y[0:48].astype(f32)
    at = pl.ds(pl.multiple_of(32 * c, 16), 16)
    acc[at] = acc[at] + xback[...].astype(f32)
    feat_own, feat_other = ordered(c, acc[:, 0:CH], acc[:, CH:WIDE])
    wide = layer[...].astype(f32)
    layer_own, layer_other = ordered(c, wide[:, 0:CH], wide[:, CH:WIDE])
    stay[0:48] = feat_own.astype(bf16)
    stay[48:80] = layer_own.astype(bf16)
    to_core[0:48] = feat_other.astype(bf16)
    to_core[48:80] = layer_other.astype(bf16)


def finish_kernel(sc, stay, from_core, read, layer_out, feat_grad, acc):
    c = sc[0]
    acc[...] = jnp.broadcast_to(read[...], (64, CH))
    mine = pl.ds(pl.multiple_of(16 * c, 16), 48)
    acc[mine] = acc[mine] + stay[0:48].astype(f32)
    other = pl.ds(pl.multiple_of(16 - 16 * c, 16), 48)
    acc[other] = acc[other] + from_core[0:48].astype(f32)
    feat_grad[...] = acc[...].astype(bf16)
    layer_out[pl.ds(pl.multiple_of(ATOMS * c, ATOMS), ATOMS)] = stay[48:80]
    layer_out[pl.ds(pl.multiple_of(ATOMS - ATOMS * c, ATOMS), ATOMS)] = from_core[48:80]


def total_kernel(sc, got, energy, forces, stress, *, atoms):
    tile = got[0]
    for s in range(1, 8):
        tile = tile + got[s]
    upper, lower, level = tile[0:1], tile[1:2], tile[2:3]
    lines = (upper, pltpu.roll(upper, 64, 1), lower, level)
    row = iota((8, CH), 0)
    lane = iota((8, CH), 1)
    here = (lane < 64) & ((lane >> 4) == (row >> 1)) & ((lane & 1) == (row & 1))
    spread = jnp.concatenate([jnp.where(here, line, 0.0) for line in lines], axis=0)
    pick = jnp.where(((iota((CH, CH), 0) >> 1) & 7) == iota((CH, CH), 1), 1.0, 0.0)
    turned = lax.dot_general(
        spread, pick, (((1,), (0,)), ((), ())), precision=HIGHEST, preferred_element_type=f32
    )
    for k in range(3):
        for r in range(4):
            r0 = 8 * k + 2 * r
            forces[k, r] = turned[r0 : r0 + 2, 0:8]
    for r in range(4):
        energy[r] = turned[24 + 2 * r : 26 + 2 * r, 0:8]
    for a in range(3):
        stress[a : a + 1] = pltpu.roll(lower, CH - 64 - 3 * a, 1)[:, 0:3] * (1.0 / atoms)


def body(
    features,
    positions,
    neighbours,
    counts,
    species,
    radial_in,
    radial_out,
    mix_weight,
    species_weight,
    out_weight,
    readout,
):
    gx = lax.axis_size("g")
    every = gx * lax.axis_size("yh")
    c = lax.axis_index("core")
    own = lax.axis_index("g")
    scalars = jnp.stack(
        [c, lax.axis_index("yh"), lax.axis_index("x"), own, (own + 2 * c - 1 + gx) % gx]
    ).astype(jnp.int32)
    meta = jnp.concatenate(
        [neighbours.reshape(64, NEIGH), counts.reshape(64, 1), species.reshape(64, 1)], axis=1
    )
    shape = jax.ShapeDtypeStruct
    send = call(send_kernel, shape((4, 64, CH), bf16))(
        scalars, features.reshape(64, CH), positions.transpose(0, 1, 3, 2)
    )
    recv = lax.all_to_all(send, ("core", "yh"), 0, 0)
    radial_out, species_weight, send = lax.optimization_barrier((radial_out, species_weight, send))
    spack = call(pack_kernel, shape((SP_ROWS, CH), bf16))(
        scalars,
        radial_out.transpose(1, 0, 2).reshape(3 * HID, CH),
        species_weight.reshape(48, CH),
        readout.reshape(1, CH),
        out_weight,
        mix_weight.reshape(3 * 1024, CH),
    )
    swap = [(0, 1), (1, 0)]
    spack_p = lax.ppermute(spack, "core", swap)
    outward = [
        (co * gx + i, (1 - co) * gx + (i - 1 + 2 * co) % gx) for co in range(2) for i in range(gx)
    ]
    edge_row = call(edge_kernel, shape((4, 32, CH), bf16), us=20.0)(scalars, recv)
    xrow = lax.ppermute(edge_row, ("core", "g"), outward)
    prep, rad, rad_t, vec, cho = call(
        prep_kernel,
        (
            shape((8, EDGES), f32),
            shape((3, HID, WIDE), bf16),
            shape((3, WIDE, HID), bf16),
            shape((16, WIDE), bf16),
            shape((8, ATOMS, WIDE), f32),
        ),
        [pltpu.VMEM((16, WIDE), f32)],
    )(scalars, meta, spack, spack_p)
    pay, geo, hidden, slope, hot, feat_t = call(
        forward_kernel,
        (
            shape((PAY, WIDE), bf16),
            shape((40, EDGES), f32),
            shape((HID, EDGES), bf16),
            shape((HID, EDGES), f32),
            shape((128, EDGES), bf16),
            shape((WIDE, 128), bf16),
        ),
        [pltpu.VMEM((MSG, WIDE), f32)],
        us=3.2,
    )(scalars, recv, xrow, prep, radial_in, rad_t, vec)
    full = lax.all_gather(pay, "x")
    back = call(mix_kernel, shape((4, SENT, WIDE), f32), us=1.7)(
        scalars, full, spack, spack_p, cho
    )
    back = lax.optimization_barrier(back.astype(jnp.float16))
    adjp = lax.optimization_barrier(lax.all_to_all(back, "x", 0, 0)).astype(f32)
    to_y, main, leaving = call(
        backward_kernel,
        (
            shape((64, WIDE), bf16),
            shape((64, WIDE), f32),
            shape((2 * every, CH), f32),
        ),
        us=4.5,
    )(scalars, hot, feat_t, geo, hidden, slope, rad, rad_t, radial_in, adjp)
    from_y = lax.ppermute(to_y, "yh", swap)
    xsend = (main[48:64] + from_y[48:64].astype(f32)).astype(bf16)
    xback = lax.ppermute(xsend, ("core", "g"), outward)
    arrived = lax.all_to_all(leaving, ("g", "yh"), 0, 0, tiled=True)
    layer, level = call(layer_kernel, (shape((ATOMS, WIDE), bf16), shape((8, CH), f32)), us=0.5)(
        scalars, recv, adjp, spack, spack_p
    )
    lines = jnp.sum(arrived.reshape(every, 2, CH), axis=0)
    tile = jnp.concatenate([lines, level[0:6]], axis=0)
    small = jnp.broadcast_to(tile[None], (8, 8, CH))
    main, small = lax.optimization_barrier((main, small))
    got = lax.all_to_all(small, ("x", "core"), 0, 0)
    stay, to_core = call(
        merge_kernel,
        (shape((80, CH), bf16), shape((80, CH), bf16)),
        [pltpu.VMEM((48, WIDE), f32)],
        us=0.05,
    )(scalars, main, from_y, xback, layer)
    from_core = lax.ppermute(to_core, "core", swap)
    layer_out, feat_grad = call(
        finish_kernel,
        (shape((64, CH), bf16), shape((64, CH), bf16)),
        [pltpu.VMEM((64, CH), f32)],
        us=0.05,
    )(scalars, stay, from_core, readout.reshape(1, CH))
    energy, forces, stress = call(
        functools.partial(total_kernel, atoms=64 * every),
        (shape((4, 2, 8), f32), shape((3, 4, 2, 8), f32), shape((3, 3), f32)),
    )(scalars, got)
    block = features.shape
    return (
        layer_out.reshape(block),
        energy.transpose(0, 2, 1),
        forces.transpose(0, 1, 3, 2),
        feat_grad.reshape(block),
        stress,
    )


def solution(mesh):
    gx = mesh.shape["gx"]
    parts = Mesh(mesh.devices.reshape(4, 2, gx, 2), ("x", "core", "g", "yh"))
    ch = ("x", "core")
    placed = (
        P("g", "yh", None, ch),
        P(None, "g", "yh", None),
        P("g", "yh", None, None),
        P("g", "yh", None),
        P("g", "yh", None),
        P(),
        P(None, None, ch),
        P(None, None, ch),
        P(None, None, ch),
        P(None, ch),
        P(ch),
    )
    return jax.shard_map(
        body,
        mesh=parts,
        in_specs=placed,
        out_specs=(
            P("g", "yh", None, ch),
            P("g", "yh", None),
            P(None, "g", "yh", None),
            P("g", "yh", None, ch),
            P(),
        ),
        check_vma=False,
    )
```

```python
import functools
import math

import jax
import jax.numpy as jnp
from jax import lax
from jax.experimental import pallas as pl
from jax.experimental.pallas import tpu as pltpu
from jax.sharding import Mesh, PartitionSpec as P

f32 = jnp.float32
bf16 = jnp.bfloat16
cutoff = 3.2
message_scale = 0.25
degree_bounds = ((0, 1), (1, 4), (4, 9))
HIGHEST = lax.Precision.HIGHEST

ATOMS = 32
NEIGH = 32
EDGES = ATOMS * NEIGH
GROUP = 1024
GROUPS = EDGES // GROUP
PER = GROUP // NEIGH
CH = 128
WIDE = 256
HID = 64
MSG = 9 * ATOMS
PAY = MSG + 16
BACK = MSG + ATOMS
SENT = BACK + 16

VMEM_LIMIT = 32 * 1024 * 1024


def nn(a, b):
    return lax.dot_general(a, b, (((1,), (0,)), ((), ())), preferred_element_type=f32)


def nt(a, b):
    return lax.dot_general(a, b, (((1,), (1,)), ((), ())), preferred_element_type=f32)


def tn(a, b):
    return lax.dot_general(a, b, (((0,), (0,)), ((), ())), preferred_element_type=f32)


def split3(v):
    hi = v.astype(bf16)
    rest = v - hi.astype(f32)
    mid = rest.astype(bf16)
    low = (rest - mid.astype(f32)).astype(bf16)
    return hi, mid, low


def split2(v):
    hi = v.astype(bf16)
    return hi, (v - hi.astype(f32)).astype(bf16)


def stacked(parts):
    return jnp.concatenate([part.astype(f32) for part in parts], axis=0)


def iota(shape, dim):
    return lax.broadcasted_iota(jnp.int32, shape, dim)


def call(kernel, out_shape, scratch=(), us=1.0, space=pltpu.VMEM, limit=VMEM_LIMIT):
    def run(scalars, *arrays):
        return pl.pallas_call(
            kernel,
            out_shape=out_shape,
            in_specs=[pl.BlockSpec(memory_space=pltpu.SMEM)]
            + [pl.BlockSpec(memory_space=space)] * len(arrays),
            out_specs=jax.tree.map(lambda _: pl.BlockSpec(memory_space=pltpu.VMEM), out_shape),
            scratch_shapes=list(scratch),
            cost_estimate=pl.CostEstimate(
                flops=int(us * 1e9), bytes_accessed=1 << 18, transcendentals=0
            ),
            compiler_params=pltpu.CompilerParams(vmem_limit_bytes=limit),
        )(scalars, *arrays)

    return run


SP_SPEC = 3 * HID
SP_READ = SP_SPEC + 144
SP_OUT = SP_READ + 16
SP_MIX = SP_OUT + 1024
SP_ROWS = SP_MIX + 3 * 1024


def send_kernel(sc, feat_any, pos_any, send, feat, pos, sems):
    copies = (
        pltpu.make_async_copy(feat_any, feat, sems.at[0]),
        pltpu.make_async_copy(pos_any, pos, sems.at[1]),
    )
    for copy in copies:
        copy.start()
    for copy in copies:
        copy.wait()
    tiles = [pos[d, r] for d in range(3) for r in range(4)]
    pick = jnp.where(((iota((8, CH), 1) >> 1) & 7) == iota((8, CH), 0), 1.0, 0.0)
    spread = lax.dot_general(
        jnp.concatenate(tiles, axis=0),
        pick,
        (((1,), (0,)), ((), ())),
        precision=HIGHEST,
        preferred_element_type=f32,
    )
    r8 = iota((8, CH), 0)
    l8 = iota((8, CH), 1)
    here = (l8 < 64) & ((l8 >> 4) == (r8 >> 1)) & ((l8 & 1) == (r8 & 1))
    lines = [
        jnp.sum(jnp.where(here, spread[8 * d : 8 * d + 8], 0.0), axis=0, keepdims=True)
        for d in range(3)
    ]
    row = iota((16, CH), 0)
    rows = jnp.zeros((16, CH), f32)
    for d in range(3):
        for k, part in enumerate(split3(lines[d])):
            rows = jnp.where(row == 3 * k + d, part.astype(f32), rows)
    for c in range(2):
        moved = (rows if c == 0 else pltpu.roll(rows, CH - 16, 1)).astype(bf16)
        for y in range(2):
            send[2 * c + y, 0:48] = feat[16 * c : 16 * c + 48]
            send[2 * c + y, 48:64] = moved


def pack_kernel(sc, rad_out, spec, read, ow, mw, spack):
    spack[SP_OUT:SP_MIX] = ow[...]
    spack[SP_MIX:SP_ROWS] = mw[...]
    spack[0:SP_SPEC] = rad_out[...]
    parts = split3(spec[...])
    for k in range(3):
        spack[SP_SPEC + 48 * k : SP_SPEC + 48 * (k + 1)] = parts[k]
    r0, r1, r2 = split3(read[...])
    rr = iota((16, CH), 0)
    rows = (
        jnp.where(rr == 0, r0.astype(f32), 0.0)
        + jnp.where(rr == 1, r1.astype(f32), 0.0)
        + jnp.where(rr == 2, r2.astype(f32), 0.0)
    )
    spack[SP_READ:SP_OUT] = rows.astype(bf16)


def edge_kernel(sc, recv, out):
    start = pl.multiple_of(32 * sc[0], 16)
    for s in range(4):
        out[s, 0:16] = recv[s, pl.ds(start, 16)]
        out[s, 16:32] = recv[s, 48:64]


def feat_table(recv, xrow, yh):
    halves = []
    for cs in range(2):
        o = 2 * cs + yh
        t = 2 * cs + 1 - yh
        halves.append(
            jnp.concatenate([recv[o, 0:48], recv[t, 0:48], xrow[o, 0:16], xrow[t, 0:16]], axis=0)
        )
    return jnp.concatenate(halves, axis=1)


def pos_table(recv, xrow, c, yh):
    lane = iota((16, CH), 1)

    def turned(value, to):
        first = pltpu.roll(value, to - 32, 1)
        return jnp.where(c == 0, first, pltpu.roll(value, to, 1))

    own = recv[yh, 48:64].astype(f32)
    across = pltpu.roll(recv[1 - yh, 48:64].astype(f32), 48, 1)
    row_own = turned(xrow[yh, 16:32].astype(f32), 96)
    row_across = turned(xrow[1 - yh, 16:32].astype(f32), 112)
    table = jnp.where(
        lane < 48, own, jnp.where(lane < 96, across, jnp.where(lane < 112, row_own, row_across))
    )
    return table.astype(bf16)


def ordered(c, own, other):
    first = jnp.where(c == 0, own, other)
    second = jnp.where(c == 0, other, own)
    return first, second


def own_index(c, start, count):
    atom = (iota((1, count), 1) >> 5) + start
    return ((atom >> 4) + c) * 16 + (atom & 15)


def prep_kernel(
    sc, meta, spk_o, spk_p, rows_ref, rad_ref, rad_t_ref, vec_ref, cho_ref, ow_ref, read_ref, tmp
):
    c = sc[0]
    start = pl.multiple_of(c * ATOMS, ATOMS)
    mine = meta[pl.ds(start, ATOMS), :]
    codes = mine[:, 0:NEIGH].astype(f32).astype(bf16)
    spread = (iota((NEIGH, EDGES), 0) == (iota((NEIGH, EDGES), 1) & 31)).astype(bf16)
    at_atom = iota((ATOMS, EDGES), 0) == (iota((ATOMS, EDGES), 1) >> 5)
    code = jnp.sum(jnp.where(at_atom, nn(codes, spread), 0.0), axis=0, keepdims=True)
    code = code.astype(jnp.int32)
    counts = mine[:, NEIGH : NEIGH + 1].astype(f32)
    count = jnp.sum(jnp.where(at_atom, counts, 0.0), axis=0, keepdims=True)
    lane = iota((1, EDGES), 1)
    slot = lane & 31
    atom = lane >> 5
    col = (atom >> 1) & 7
    third = (code * 43) >> 8
    step_x = third - 1
    step_y = (code >> 1) - 3 * third - 1
    q = (atom >> 4) + step_x + c
    y = col + step_y
    across = jnp.where((y < 0) | (y > 7), 1, 0)
    inside = (q >= 0) & (q <= 2)
    idx = (
        jnp.where(inside, across * 48 + q * 16, 96 + across * 16) + (y & 7) * 2 + (code & 1)
    )
    rows_ref[0:1] = idx.astype(f32)
    rows_ref[1:2] = jnp.where(slot.astype(f32) < count, message_scale, 0.0)
    rows_ref[2:3] = step_x.astype(f32)
    rows_ref[3:4] = step_y.astype(f32)
    rows_ref[4:8] = jnp.zeros((4, EDGES), f32)
    for degree in range(3):
        rows = slice(degree * HID, (degree + 1) * HID)
        first, second = ordered(c, spk_o[rows].astype(f32), spk_p[rows].astype(f32))
        wide = jnp.concatenate([first, second], axis=1)
        rad_ref[degree] = wide.astype(bf16)
        rad_t_ref[degree] = wide.T.astype(bf16)
    ow_ref[...] = jnp.concatenate([spk_o[SP_OUT:SP_MIX], spk_p[SP_OUT:SP_MIX]], axis=1)
    ra, rb = ordered(
        c, spk_o[SP_READ:SP_OUT].astype(f32), spk_p[SP_READ:SP_OUT].astype(f32)
    )
    read = jnp.concatenate([ra, rb], axis=1)
    read_ref[...] = jnp.broadcast_to(read[0:1] + read[1:2] + read[2:3], (8, WIDE))
    vec = 0.0
    for ref in (spk_o, spk_p):
        vec = vec + nt(ref[SP_READ:SP_OUT], ref[SP_OUT:SP_MIX])
    vec = vec[0:1] + vec[1:2] + vec[2:3]
    tmp[...] = jnp.zeros((16, WIDE), f32)
    for b in range(4):
        parts = split3(vec[:, b * WIDE : (b + 1) * WIDE])
        for k in range(3):
            tmp[3 * b + k : 3 * b + k + 1] = parts[k].astype(f32)
    vec_ref[...] = tmp[...].astype(bf16)
    species = mine[:, NEIGH + 1 : NEIGH + 2]
    whole = []
    for ref in (spk_o, spk_p):
        whole.append(
            sum(ref[SP_SPEC + 48 * k : SP_SPEC + 48 * (k + 1)].astype(f32) for k in (2, 1, 0))
        )
    spec = jnp.concatenate(whole, axis=1)
    for t in range(8):
        value = jnp.zeros((ATOMS, WIDE), f32)
        for s in range(6):
            value = jnp.where(species == s, spec[8 * s + t : 8 * s + t + 1], value)
        cho_ref[t] = value


def forward_kernel(
    sc, recv, xrow, prep, rad_in, rad_t, vec, pay, geo, hid_ref, slope, hot_ref, feat_ref, acc
):
    c = sc[0]
    yh = sc[1]
    idx = prep[0:1].astype(jnp.int32)
    scaled = prep[1:2]
    rows = iota((128, EDGES), 0)
    hot = jnp.where(rows == idx, 1.0, 0.0)
    diff = (hot - jnp.where(rows == own_index(c, 0, EDGES), 1.0, 0.0)).astype(bf16)
    moved = nn(pos_table(recv, xrow, c, yh), diff)
    rel = moved[0:3] + moved[3:6] + moved[6:9]
    rx = prep[2:3] + rel[0:1]
    ry = prep[3:4] + rel[1:2]
    rz = rel[2:3]
    rho = jnp.sqrt(rx * rx + ry * ry + rz * rz + 0.25)
    inv = 1.0 / rho
    ux, uy, uz = rx * inv, ry * inv, rz * inv
    ratio = rho / cutoff
    theta = math.pi * ratio
    gap = 1.0 - ratio * ratio
    env = gap * gap * inv
    turns = (iota((8, 1), 0) + 1).astype(f32) * theta
    sins = jnp.sin(turns)
    geo[0:1] = idx.astype(f32)
    geo[1:2] = scaled
    geo[2:3] = rx
    geo[3:4] = ry
    geo[4:5] = rz
    geo[5:6] = rho
    geo[6:7] = inv
    geo[7:8] = env
    geo[8:16] = sins
    geo[16:24] = jnp.cos(turns)
    basis = sins * env
    r_hi, r_mid, r_lo = split3(rad_in[...])
    b_hi, b_mid, b_lo = split3(basis)
    z = tn(
        stacked((r_hi, r_hi, r_mid, r_hi, r_lo, r_mid)).astype(bf16),
        stacked((b_hi, b_mid, b_hi, b_lo, b_hi, b_mid)).astype(bf16),
    )
    sig = lax.logistic(z)
    hidden = (z * sig).astype(bf16)
    hid_ref[...] = hidden
    slope[...] = sig * (1.0 + z * (1.0 - sig))
    harm = (
        scaled,
        scaled * ux,
        scaled * uy,
        scaled * uz,
        scaled * ux * uy,
        scaled * uy * uz,
        scaled * (1.5 * uz * uz - 0.5),
        scaled * ux * uz,
        scaled * 0.5 * (ux * ux - uy * uy),
    )
    for m in range(9):
        geo[24 + m : 25 + m] = harm[m]
    feat_t = feat_table(recv, xrow, yh).astype(f32).T.astype(bf16)
    block = iota((PER, GROUP), 0) == (iota((PER, GROUP), 1) >> 5)
    hot_b = hot.astype(bf16)
    hot_ref[...] = hot_b
    feat_ref[...] = feat_t
    for g in range(GROUPS):
        at = slice(g * GROUP, (g + 1) * GROUP)
        nb = nn(feat_t, hot_b[:, at])
        hid = hidden[:, at]
        radials = nn(rad_t[...].reshape(3 * WIDE, HID), hid)
        for degree, (first, last) in enumerate(degree_bounds):
            p_hi, p_lo = split2(radials[degree * WIDE : (degree + 1) * WIDE] * nb)
            blocks = [jnp.where(block, harm[m][:, at], 0.0) for m in range(first, last)]
            y_hi, y_lo = split2(jnp.concatenate(blocks, axis=0))
            both = nt(jnp.concatenate([y_hi, y_lo], axis=0), p_hi)
            half = (last - first) * PER
            msg = both[:half] + both[half:] + nt(y_hi, p_lo)
            for k in range(last - first):
                r0 = (first + k) * ATOMS + g * PER
                acc[r0 : r0 + PER] = msg[k * PER : (k + 1) * PER]
    pay[0:MSG] = acc[0:MSG].astype(bf16)
    pay[MSG:PAY] = vec[...]


TOP = 14.0


def level_of(value):
    peak = jnp.max(jnp.max(jnp.abs(value), axis=0, keepdims=True), axis=1, keepdims=True)
    return jnp.clip(jnp.floor(jnp.log2(jnp.maximum(peak, 1e-30))), -100.0, 100.0)


def scale_of(adjp, s, row):
    return jnp.exp2(adjp[s, BACK + row : BACK + row + 1, 0:1] - TOP)


def mix_of(spk_o, spk_p, degree):
    at = slice(SP_MIX + 1024 * degree, SP_MIX + 1024 * (degree + 1))
    return jnp.concatenate([spk_o[at], spk_p[at]], axis=1)


def mix_kernel(sc, full, spk_o, spk_p, cho, out):
    c = sc[0]
    x = sc[2]
    at = (iota((16, WIDE), 0) * 43) >> 7
    tall = jnp.zeros((16, WIDE), f32)
    for s in range(4):
        tall = tall + full[s, MSG:PAY, :].astype(f32)
    vec = jnp.sum(jnp.where(at == x, tall, 0.0), axis=0, keepdims=True)
    vec_o, vec_p = ordered(c, vec[:, 0:CH], vec[:, CH:WIDE])
    vec = jnp.concatenate([vec_o, vec_p], axis=1)
    mixed = []
    for degree, (first, last) in enumerate(degree_bounds):
        rows = slice(first * ATOMS, last * ATOMS)
        lhs = jnp.concatenate([full[s, rows, :] for s in range(4)], axis=1)
        both = nn(lhs, mix_of(spk_o, spk_p, degree))
        for m in range(last - first):
            mixed.append(both[m * ATOMS : (m + 1) * ATOMS])

    chosen = [cho[t] for t in range(8)]
    cen, ax, ay, az, qa, qb, qc, qd, qe = mixed
    vec_sq = ax * ax + ay * ay + az * az
    quad_sq = qa * qa + qb * qb + qc * qc + qd * qd + qe * qe
    up = qe - qc
    down = qe + qc
    cubic = (
        up * ax * ax
        - down * ay * ay
        + 2.0 * qc * az * az
        + 2.0 * (qa * ax * ay + qb * ay * az + qd * ax * az)
    )
    cen_sq = cen * cen
    products = (
        cen * chosen[0]
        + cen_sq * chosen[1]
        + vec_sq * chosen[2]
        + quad_sq * chosen[3]
        + cen_sq * cen * chosen[4]
        + cen * vec_sq * chosen[5]
        + cen * quad_sq * chosen[6]
        + cubic * chosen[7]
    )
    first, second = ordered(c, products[:, 0:CH], products[:, CH:WIDE])
    prod = jnp.concatenate([first, second], axis=1).astype(bf16).astype(f32)
    w = [vec * value for value in chosen]
    a_scale = 2.0 * (w[2] + cen * w[5])
    q_scale = 2.0 * (w[3] + cen * w[6])
    w7 = w[7]
    tw7 = 2.0 * w7
    grads = [
        w[0] + 2.0 * cen * w[1] + 3.0 * cen_sq * w[4] + vec_sq * w[5] + quad_sq * w[6],
        a_scale * ax + tw7 * (up * ax + qa * ay + qd * az),
        a_scale * ay + tw7 * (qa * ax - down * ay + qb * az),
        a_scale * az + tw7 * (2.0 * qc * az + qb * ay + qd * ax),
        q_scale * qa + tw7 * ax * ay,
        q_scale * qb + tw7 * ay * az,
        q_scale * qc + w7 * (2.0 * az * az - ax * ax - ay * ay),
        q_scale * qd + tw7 * ax * az,
        q_scale * qe + w7 * (ax * ax - ay * ay),
    ]
    backs = []
    for degree, (first, last) in enumerate(degree_bounds):
        adj = jnp.concatenate(grads[first:last], axis=0).astype(bf16)
        backs.append(nt(adj, mix_of(spk_o, spk_p, degree)))
    back = jnp.concatenate(backs, axis=0)
    level_back, level_prod = level_of(back), level_of(prod)
    back = back * jnp.exp2(TOP - level_back)
    prod = prod * jnp.exp2(TOP - level_prod)
    row = iota((16, WIDE), 0)
    levels = jnp.where(row == 0, level_back, jnp.where(row == 1, level_prod, 0.0))
    for s in range(4):
        out[s, 0:MSG, :] = back[:, s * WIDE : (s + 1) * WIDE]
        out[s, MSG:BACK, :] = prod
        out[s, BACK:SENT, :] = levels


def backward_kernel(
    sc, hot, feat_t, geo, hidden, slope, rad, rad_t, rad_in, adjp, to_y, main, out
):
    c = sc[0]
    yh = sc[1]
    adjm = adjp[0, 0:MSG, :] * scale_of(adjp, 0, 0)
    for s in range(1, 4):
        adjm = adjm + adjp[s, 0:MSG, :] * scale_of(adjp, s, 0)
    r_hi, r_lo = split2(rad_in[...])
    outer = jnp.concatenate([r_hi, r_hi, r_lo], axis=1)
    order = (iota((8, 1), 0) + 1).astype(f32)
    r8 = iota((8, GROUP), 0)
    rows = iota((128, GROUP), 0)
    block = iota((PER, GROUP), 0) == (iota((PER, GROUP), 1) >> 5)

    def rows_of(x, y, z):
        return jnp.where(r8 == 0, x, jnp.where(r8 == 1, y, jnp.where(r8 == 2, z, 0.0)))

    feats = jnp.zeros((128, WIDE), f32)
    found = jnp.zeros((24, CH + 32), f32)
    for g in range(GROUPS):
        at = slice(g * GROUP, (g + 1) * GROUP)
        hot_g = hot[:, at]
        nb = nn(feat_t[...], hot_g)
        hid = hidden[:, at]
        radials = nn(rad_t[...].reshape(3 * WIDE, HID), hid)
        gh = jnp.zeros((HID, GROUP), f32)
        fb = jnp.zeros((WIDE, GROUP), f32)
        gys = []
        scaled = geo[1:2, at]
        for degree, (first, last) in enumerate(degree_bounds):
            radial = radials[degree * WIDE : (degree + 1) * WIDE]
            prod = (radial * nb).astype(bf16)
            blocks = [jnp.where(block, geo[24 + m : 25 + m, at], 0.0) for m in range(first, last)]
            y_hi, y_lo = split2(jnp.concatenate(blocks, axis=0))
            pieces = [
                adjm[m * ATOMS + g * PER : m * ATOMS + (g + 1) * PER] for m in range(first, last)
            ]
            a_hi, a_lo = split2(jnp.concatenate(pieces, axis=0))
            grad_prod = tn(
                jnp.concatenate([a_hi, a_lo, a_hi], axis=0),
                jnp.concatenate([y_hi, y_hi, y_lo], axis=0),
            )
            both = nn(jnp.concatenate([a_hi, a_lo], axis=0), prod)
            half = (last - first) * PER
            over = both[:half] + both[half:]
            for k in range(last - first):
                part = jnp.where(block, over[k * PER : (k + 1) * PER], 0.0)
                gys.append(scaled * jnp.sum(part, axis=0, keepdims=True))
            gh = gh + nn(rad[degree], (grad_prod * nb).astype(bf16))
            fb = fb + grad_prod * radial
        feats = feats + nt(hot_g, fb.astype(bf16))
        rx, ry, rz = geo[2:3, at], geo[3:4, at], geo[4:5, at]
        rho, inv, env = geo[5:6, at], geo[6:7, at], geo[7:8, at]
        d_hi, d_lo = split2(gh * slope[:, at])
        dbasis = nn(outer, jnp.concatenate([d_hi, d_lo, d_hi], axis=0))
        ratio = rho / cutoff
        gap = 1.0 - ratio * ratio
        by_cos = jnp.sum(dbasis * order * geo[16:24, at], axis=0, keepdims=True)
        by_sin = jnp.sum(dbasis * geo[8:16, at], axis=0, keepdims=True)
        drho = by_cos * (math.pi / cutoff) * env - by_sin * inv * (
            env + (4.0 / cutoff) * ratio * gap
        )
        ux, uy, uz = rx * inv, ry * inv, rz * inv
        gx_ = gys[1] + gys[4] * uy + gys[7] * uz + gys[8] * ux
        gy_ = gys[2] + gys[4] * ux + gys[5] * uz - gys[8] * uy
        gz_ = gys[3] + gys[5] * uy + 3.0 * gys[6] * uz + gys[7] * ux
        along = drho - (gx_ * ux + gy_ * uy + gz_ * uz) * inv
        eg = rows_of(gx_ * inv + ux * along, gy_ * inv + uy * along, gz_ * inv + uz * along)
        diff = jnp.where(rows == own_index(c, g * PER, GROUP), 1.0, 0.0) - hot_g.astype(f32)
        places = stacked(split3(rows_of(rx, ry, rz)) + (jnp.zeros((8, GROUP), f32),))
        against = jnp.concatenate([diff, places], axis=0).astype(bf16)
        found = found + nt(stacked(split3(eg)).astype(bf16), against)
    main[0:48] = feats[0:48]
    main[48:64] = feats[96:112]
    to_y[0:48] = feats[48:96].astype(bf16)
    to_y[48:64] = feats[112:128].astype(bf16)
    found = found[0:8] + found[8:16] + found[16:24]
    force = found[:, 0:CH]
    lane = iota((1, CH), 1)
    cross = jnp.concatenate([found[:, CH : CH + 32], jnp.zeros((8, CH - 32), f32)], axis=1)
    cross = cross + pltpu.roll(cross, CH - 8, 1) + pltpu.roll(cross, CH - 16, 1)
    virial = jnp.zeros((1, CH), f32)
    for a in range(3):
        for b in range(3):
            to = 64 + 3 * a + b
            virial = jnp.where(lane == to, pltpu.roll(cross, to - a, 1)[b : b + 1], virial)

    def placed(first, count, to):
        moved = force if to == first else pltpu.roll(force, (to - first) % CH, 1)
        return jnp.where((lane >= to) & (lane < to + count), moved, 0.0)

    def by_core(first, count, to_0, to_1):
        return jnp.where(c == 0, placed(first, count, to_0), placed(first, count, to_1))

    own, beside = sc[3], sc[4]
    goals = (
        (2 * own + yh, by_core(0, 48, 0, 16)),
        (2 * own + 1 - yh, by_core(48, 48, 0, 16)),
        (2 * beside + yh, by_core(96, 16, 48, 0)),
        (2 * beside + 1 - yh, by_core(112, 16, 48, 0)),
    )
    row = iota(out.shape, 0)
    odd = (row & 1) == 1
    total = jnp.where(odd, virial, 0.0)
    for device, value in goals:
        upper = value[0:1] + pltpu.roll(value, 64, 1)[1:2]
        chunk = jnp.where(odd, value[2:3], upper)
        total = total + jnp.where((row >> 1) == device, chunk, 0.0)
    out[...] = total


def layer_kernel(sc, recv, adjp, weights, read, layer_ref, level_ref):
    c = sc[0]
    yh = sc[1]
    parts = [adjp[s, MSG:BACK, :] * scale_of(adjp, s, 1) for s in range(4)]
    both = nn(jnp.concatenate(parts, axis=1).astype(bf16), weights[...])
    first, second = ordered(c, both[:, 0:CH], both[:, CH:WIDE])
    start = pl.multiple_of(c * 16, 16)
    own_feat = jnp.concatenate(
        [recv[2 * cs + yh, pl.ds(start, ATOMS), :].astype(f32) for cs in range(2)], axis=1
    )
    layer = jnp.concatenate([first, second], axis=1) + own_feat
    layer_ref[...] = layer.astype(bf16)
    energy = jnp.sum(layer * read[0:1], axis=1, keepdims=True)
    lane = iota((ATOMS, CH), 1)
    row = iota((ATOMS, CH), 0)
    level = jnp.sum(jnp.where(lane == row + ATOMS * c, energy, 0.0), axis=0, keepdims=True)
    level_ref[...] = jnp.broadcast_to(level, (8, CH))


def merge_kernel(sc, main, from_y, xback, layer, stay, to_core, acc):
    c = sc[0]
    acc[...] = main[0:48] + from_y[0:48].astype(f32)
    at = pl.ds(pl.multiple_of(32 * c, 16), 16)
    acc[at] = acc[at] + xback[...].astype(f32)
    feat_own, feat_other = ordered(c, acc[:, 0:CH], acc[:, CH:WIDE])
    wide = layer[...].astype(f32)
    layer_own, layer_other = ordered(c, wide[:, 0:CH], wide[:, CH:WIDE])
    stay[0:48] = feat_own.astype(bf16)
    stay[48:80] = layer_own.astype(bf16)
    to_core[0:48] = feat_other.astype(bf16)
    to_core[48:80] = layer_other.astype(bf16)


def finish_kernel(
    sc, stay, from_core, read, got, layer_out, feat_grad, energy, forces, stress, acc, *, atoms
):
    c = sc[0]
    acc[...] = jnp.broadcast_to(read[...], (64, CH))
    mine = pl.ds(pl.multiple_of(16 * c, 16), 48)
    acc[mine] = acc[mine] + stay[0:48].astype(f32)
    other = pl.ds(pl.multiple_of(16 - 16 * c, 16), 48)
    acc[other] = acc[other] + from_core[0:48].astype(f32)
    feat_grad[...] = acc[...].astype(bf16)
    layer_out[pl.ds(pl.multiple_of(ATOMS * c, ATOMS), ATOMS)] = stay[48:80]
    layer_out[pl.ds(pl.multiple_of(ATOMS - ATOMS * c, ATOMS), ATOMS)] = from_core[48:80]
    tile = got[0]
    for s in range(1, 8):
        tile = tile + got[s]
    upper, lower, level = tile[0:1], tile[1:2], tile[2:3]
    lines = (upper, pltpu.roll(upper, 64, 1), lower, level)
    row = iota((8, CH), 0)
    lane = iota((8, CH), 1)
    here = (lane < 64) & ((lane >> 4) == (row >> 1)) & ((lane & 1) == (row & 1))
    spread = jnp.concatenate([jnp.where(here, line, 0.0) for line in lines], axis=0)
    pick = jnp.where(((iota((CH, CH), 0) >> 1) & 7) == iota((CH, CH), 1), 1.0, 0.0)
    turned = lax.dot_general(
        spread, pick, (((1,), (0,)), ((), ())), precision=HIGHEST, preferred_element_type=f32
    )
    for k in range(3):
        for r in range(4):
            r0 = 8 * k + 2 * r
            forces[k, r] = turned[r0 : r0 + 2, 0:8]
    for r in range(4):
        energy[r] = turned[24 + 2 * r : 26 + 2 * r, 0:8]
    for a in range(3):
        stress[a : a + 1] = pltpu.roll(lower, CH - 64 - 3 * a, 1)[:, 0:3] * (1.0 / atoms)


def body(
    features,
    positions,
    neighbours,
    counts,
    species,
    radial_in,
    radial_out,
    mix_weight,
    species_weight,
    out_weight,
    readout,
):
    gx = lax.axis_size("g")
    every = gx * lax.axis_size("yh")
    c = lax.axis_index("core")
    own = lax.axis_index("g")
    scalars = jnp.stack(
        [c, lax.axis_index("yh"), lax.axis_index("x"), own, (own + 2 * c - 1 + gx) % gx]
    ).astype(jnp.int32)
    meta = jnp.concatenate(
        [neighbours.reshape(64, NEIGH), counts.reshape(64, 1), species.reshape(64, 1)], axis=1
    )
    shape = jax.ShapeDtypeStruct
    send = call(
        send_kernel,
        shape((4, 64, CH), bf16),
        [
            pltpu.VMEM((64, CH), bf16),
            pltpu.VMEM((3, 4, 2, 8), f32),
            pltpu.SemaphoreType.DMA((2,)),
        ],
        space=pl.ANY,
        limit=63 * 1024 * 1024,
    )(
        scalars, features.reshape(64, CH), positions.transpose(0, 1, 3, 2)
    )
    recv = lax.all_to_all(send, ("core", "yh"), 0, 0)
    radial_out, species_weight, send = lax.optimization_barrier((radial_out, species_weight, send))
    spack = call(pack_kernel, shape((SP_ROWS, CH), bf16))(
        scalars,
        radial_out.transpose(1, 0, 2).reshape(3 * HID, CH),
        species_weight.reshape(48, CH),
        readout.reshape(1, CH),
        out_weight,
        mix_weight.reshape(3 * 1024, CH),
    )
    swap = [(0, 1), (1, 0)]
    spack_p = lax.ppermute(spack, "core", swap)
    outward = [
        (co * gx + i, (1 - co) * gx + (i - 1 + 2 * co) % gx) for co in range(2) for i in range(gx)
    ]
    edge_row = call(edge_kernel, shape((4, 32, CH), bf16), us=20.0)(scalars, recv)
    xrow = lax.ppermute(edge_row, ("core", "g"), outward)
    prep, rad, rad_t, vec, cho, wide_out, wide_read = call(
        prep_kernel,
        (
            shape((8, EDGES), f32),
            shape((3, HID, WIDE), bf16),
            shape((3, WIDE, HID), bf16),
            shape((16, WIDE), bf16),
            shape((8, ATOMS, WIDE), f32),
            shape((1024, WIDE), bf16),
            shape((8, WIDE), f32),
        ),
        [pltpu.VMEM((16, WIDE), f32)],
    )(scalars, meta, spack, spack_p)
    pay, geo, hidden, slope, hot, feat_t = call(
        forward_kernel,
        (
            shape((PAY, WIDE), bf16),
            shape((40, EDGES), f32),
            shape((HID, EDGES), bf16),
            shape((HID, EDGES), f32),
            shape((128, EDGES), bf16),
            shape((WIDE, 128), bf16),
        ),
        [pltpu.VMEM((MSG, WIDE), f32)],
        us=3.2,
    )(scalars, recv, xrow, prep, radial_in, rad_t, vec)
    full = lax.all_gather(pay, "x")
    back = call(mix_kernel, shape((4, SENT, WIDE), f32), us=1.7)(
        scalars, full, spack, spack_p, cho
    )
    back = lax.optimization_barrier(back.astype(jnp.float16))
    adjp = lax.optimization_barrier(lax.all_to_all(back, "x", 0, 0)).astype(f32)
    to_y, main, leaving = call(
        backward_kernel,
        (
            shape((64, WIDE), bf16),
            shape((64, WIDE), f32),
            shape((2 * every, CH), f32),
        ),
        us=4.5,
    )(scalars, hot, feat_t, geo, hidden, slope, rad, rad_t, radial_in, adjp)
    from_y = lax.ppermute(to_y, "yh", swap)
    xsend = (main[48:64] + from_y[48:64].astype(f32)).astype(bf16)
    xback = lax.ppermute(xsend, ("core", "g"), outward)
    arrived = lax.all_to_all(leaving, ("g", "yh"), 0, 0, tiled=True)
    layer, level = call(layer_kernel, (shape((ATOMS, WIDE), bf16), shape((8, CH), f32)), us=0.5)(
        scalars, recv, adjp, wide_out, wide_read
    )
    lines = jnp.sum(arrived.reshape(every, 2, CH), axis=0)
    tile = jnp.concatenate([lines, level[0:6]], axis=0)
    small = jnp.broadcast_to(tile[None], (8, 8, CH))
    main, small = lax.optimization_barrier((main, small))
    got = lax.all_to_all(small, ("x", "core"), 0, 0)
    stay, to_core = call(
        merge_kernel,
        (shape((80, CH), bf16), shape((80, CH), bf16)),
        [pltpu.VMEM((48, WIDE), f32)],
        us=0.05,
    )(scalars, main, from_y, xback, layer)
    from_core = lax.ppermute(to_core, "core", swap)
    layer_out, feat_grad, energy, forces, stress = call(
        functools.partial(finish_kernel, atoms=64 * every),
        (
            shape((64, CH), bf16),
            shape((64, CH), bf16),
            shape((4, 2, 8), f32),
            shape((3, 4, 2, 8), f32),
            shape((3, 3), f32),
        ),
        [pltpu.VMEM((64, CH), f32)],
        us=0.05,
    )(scalars, stay, from_core, readout.reshape(1, CH), got)
    block = features.shape
    return (
        layer_out.reshape(block),
        energy.transpose(0, 2, 1),
        forces.transpose(0, 1, 3, 2),
        feat_grad.reshape(block),
        stress,
    )


def solution(mesh):
    gx = mesh.shape["gx"]
    parts = Mesh(mesh.devices.reshape(4, 2, gx, 2), ("x", "core", "g", "yh"))
    ch = ("x", "core")
    placed = (
        P("g", "yh", None, ch),
        P(None, "g", "yh", None),
        P("g", "yh", None, None),
        P("g", "yh", None),
        P("g", "yh", None),
        P(),
        P(None, None, ch),
        P(None, None, ch),
        P(None, None, ch),
        P(None, ch),
        P(ch),
    )
    return jax.shard_map(
        body,
        mesh=parts,
        in_specs=placed,
        out_specs=(
            P("g", "yh", None, ch),
            P("g", "yh", None),
            P(None, "g", "yh", None),
            P("g", "yh", None, ch),
            P(),
        ),
        check_vma=False,
    )
```

```python
import functools
import math

import jax
import jax.numpy as jnp
from jax import lax
from jax.experimental import pallas as pl
from jax.experimental.pallas import tpu as pltpu
from jax.sharding import Mesh, PartitionSpec as P

f32 = jnp.float32
bf16 = jnp.bfloat16
cutoff = 3.2
message_scale = 0.25
degree_bounds = ((0, 1), (1, 4), (4, 9))
HIGHEST = lax.Precision.HIGHEST

ATOMS = 32
NEIGH = 32
EDGES = ATOMS * NEIGH
GROUP = 1024
GROUPS = EDGES // GROUP
PER = GROUP // NEIGH
CH = 128
WIDE = 256
HID = 64
MSG = 9 * ATOMS
PAY = MSG + 16
BACK = MSG + ATOMS
SENT = BACK + 16

VMEM_LIMIT = 48 * 1024 * 1024


def nn(a, b):
    return lax.dot_general(a, b, (((1,), (0,)), ((), ())), preferred_element_type=f32)


def nt(a, b):
    return lax.dot_general(a, b, (((1,), (1,)), ((), ())), preferred_element_type=f32)


def tn(a, b):
    return lax.dot_general(a, b, (((0,), (0,)), ((), ())), preferred_element_type=f32)


def split3(v):
    hi = v.astype(bf16)
    rest = v - hi.astype(f32)
    mid = rest.astype(bf16)
    low = (rest - mid.astype(f32)).astype(bf16)
    return hi, mid, low


def split2(v):
    hi = v.astype(bf16)
    return hi, (v - hi.astype(f32)).astype(bf16)


def stacked(parts):
    return jnp.concatenate([part.astype(f32) for part in parts], axis=0)


def iota(shape, dim):
    return lax.broadcasted_iota(jnp.int32, shape, dim)


def call(kernel, out_shape, scratch=(), us=1.0):
    def run(scalars, *arrays):
        return pl.pallas_call(
            kernel,
            out_shape=out_shape,
            in_specs=[pl.BlockSpec(memory_space=pltpu.SMEM)]
            + [pl.BlockSpec(memory_space=pltpu.VMEM)] * len(arrays),
            out_specs=jax.tree.map(lambda _: pl.BlockSpec(memory_space=pltpu.VMEM), out_shape),
            scratch_shapes=list(scratch),
            cost_estimate=pl.CostEstimate(
                flops=int(us * 1e9), bytes_accessed=1 << 18, transcendentals=0
            ),
            compiler_params=pltpu.CompilerParams(vmem_limit_bytes=VMEM_LIMIT),
        )(scalars, *arrays)

    return run


SP_SPEC = 3 * HID
SP_READ = SP_SPEC + 144
SP_OUT = SP_READ + 16
SP_MIX = SP_OUT + 1024
SP_ROWS = SP_MIX + 3 * 1024


def send_kernel(sc, feat, pos, send):
    tiles = [pos[d, r] for d in range(3) for r in range(4)]
    pick = jnp.where(((iota((8, CH), 1) >> 1) & 7) == iota((8, CH), 0), 1.0, 0.0)
    spread = lax.dot_general(
        jnp.concatenate(tiles, axis=0),
        pick,
        (((1,), (0,)), ((), ())),
        precision=HIGHEST,
        preferred_element_type=f32,
    )
    r8 = iota((8, CH), 0)
    l8 = iota((8, CH), 1)
    here = (l8 < 64) & ((l8 >> 4) == (r8 >> 1)) & ((l8 & 1) == (r8 & 1))
    lines = [
        jnp.sum(jnp.where(here, spread[8 * d : 8 * d + 8], 0.0), axis=0, keepdims=True)
        for d in range(3)
    ]
    row = iota((16, CH), 0)
    rows = jnp.zeros((16, CH), f32)
    for d in range(3):
        for k, part in enumerate(split3(lines[d])):
            rows = jnp.where(row == 3 * k + d, part.astype(f32), rows)
    for c in range(2):
        moved = (rows if c == 0 else pltpu.roll(rows, CH - 16, 1)).astype(bf16)
        for y in range(2):
            send[2 * c + y, 0:48] = feat[16 * c : 16 * c + 48]
            send[2 * c + y, 48:64] = moved


def pack_kernel(sc, rad_out, spec, read, ow, mw, spack):
    spack[SP_OUT:SP_MIX] = ow[...]
    spack[SP_MIX:SP_ROWS] = mw[...]
    spack[0:SP_SPEC] = rad_out[...]
    parts = split3(spec[...])
    for k in range(3):
        spack[SP_SPEC + 48 * k : SP_SPEC + 48 * (k + 1)] = parts[k]
    r0, r1, r2 = split3(read[...])
    rr = iota((16, CH), 0)
    rows = (
        jnp.where(rr == 0, r0.astype(f32), 0.0)
        + jnp.where(rr == 1, r1.astype(f32), 0.0)
        + jnp.where(rr == 2, r2.astype(f32), 0.0)
    )
    spack[SP_READ:SP_OUT] = rows.astype(bf16)


def edge_kernel(sc, recv, out):
    start = pl.multiple_of(32 * sc[0], 16)
    for s in range(4):
        out[s, 0:16] = recv[s, pl.ds(start, 16)]
        out[s, 16:32] = recv[s, 48:64]


def feat_table(recv, xrow, yh):
    halves = []
    for cs in range(2):
        o = 2 * cs + yh
        t = 2 * cs + 1 - yh
        halves.append(
            jnp.concatenate([recv[o, 0:48], recv[t, 0:48], xrow[o, 0:16], xrow[t, 0:16]], axis=0)
        )
    return jnp.concatenate(halves, axis=1)


def pos_table(recv, xrow, c, yh):
    lane = iota((16, CH), 1)

    def turned(value, to):
        first = pltpu.roll(value, to - 32, 1)
        return jnp.where(c == 0, first, pltpu.roll(value, to, 1))

    own = recv[yh, 48:64].astype(f32)
    across = pltpu.roll(recv[1 - yh, 48:64].astype(f32), 48, 1)
    row_own = turned(xrow[yh, 16:32].astype(f32), 96)
    row_across = turned(xrow[1 - yh, 16:32].astype(f32), 112)
    table = jnp.where(
        lane < 48, own, jnp.where(lane < 96, across, jnp.where(lane < 112, row_own, row_across))
    )
    return table.astype(bf16)


def ordered(c, own, other):
    first = jnp.where(c == 0, own, other)
    second = jnp.where(c == 0, other, own)
    return first, second


def own_index(c, start, count):
    atom = (iota((1, count), 1) >> 5) + start
    return ((atom >> 4) + c) * 16 + (atom & 15)


def prep_kernel(
    sc, meta, spk_o, spk_p, rows_ref, rad_ref, rad_t_ref, vec_ref, cho_ref, ow_ref, read_ref, tmp
):
    c = sc[0]
    start = pl.multiple_of(c * ATOMS, ATOMS)
    mine = meta[pl.ds(start, ATOMS), :]
    codes = mine[:, 0:NEIGH].astype(f32).astype(bf16)
    spread = (iota((NEIGH, EDGES), 0) == (iota((NEIGH, EDGES), 1) & 31)).astype(bf16)
    at_atom = iota((ATOMS, EDGES), 0) == (iota((ATOMS, EDGES), 1) >> 5)
    code = jnp.sum(jnp.where(at_atom, nn(codes, spread), 0.0), axis=0, keepdims=True)
    code = code.astype(jnp.int32)
    counts = mine[:, NEIGH : NEIGH + 1].astype(f32)
    count = jnp.sum(jnp.where(at_atom, counts, 0.0), axis=0, keepdims=True)
    lane = iota((1, EDGES), 1)
    slot = lane & 31
    atom = lane >> 5
    col = (atom >> 1) & 7
    third = (code * 43) >> 8
    step_x = third - 1
    step_y = (code >> 1) - 3 * third - 1
    q = (atom >> 4) + step_x + c
    y = col + step_y
    across = jnp.where((y < 0) | (y > 7), 1, 0)
    inside = (q >= 0) & (q <= 2)
    idx = (
        jnp.where(inside, across * 48 + q * 16, 96 + across * 16) + (y & 7) * 2 + (code & 1)
    )
    rows_ref[0:1] = idx.astype(f32)
    rows_ref[1:2] = jnp.where(slot.astype(f32) < count, message_scale, 0.0)
    rows_ref[2:3] = step_x.astype(f32)
    rows_ref[3:4] = step_y.astype(f32)
    rows_ref[4:8] = jnp.zeros((4, EDGES), f32)
    for degree in range(3):
        rows = slice(degree * HID, (degree + 1) * HID)
        first, second = ordered(c, spk_o[rows].astype(f32), spk_p[rows].astype(f32))
        wide = jnp.concatenate([first, second], axis=1)
        rad_ref[degree] = wide.astype(bf16)
        rad_t_ref[degree] = wide.T.astype(bf16)
    ow_ref[...] = jnp.concatenate([spk_o[SP_OUT:SP_MIX], spk_p[SP_OUT:SP_MIX]], axis=1)
    ra, rb = ordered(
        c, spk_o[SP_READ:SP_OUT].astype(f32), spk_p[SP_READ:SP_OUT].astype(f32)
    )
    read = jnp.concatenate([ra, rb], axis=1)
    read_ref[...] = jnp.broadcast_to(read[0:1] + read[1:2] + read[2:3], (8, WIDE))
    vec = 0.0
    for ref in (spk_o, spk_p):
        vec = vec + nt(ref[SP_READ:SP_OUT], ref[SP_OUT:SP_MIX])
    vec = vec[0:1] + vec[1:2] + vec[2:3]
    tmp[...] = jnp.zeros((16, WIDE), f32)
    for b in range(4):
        parts = split3(vec[:, b * WIDE : (b + 1) * WIDE])
        for k in range(3):
            tmp[3 * b + k : 3 * b + k + 1] = parts[k].astype(f32)
    vec_ref[...] = tmp[...].astype(bf16)
    species = mine[:, NEIGH + 1 : NEIGH + 2]
    whole = []
    for ref in (spk_o, spk_p):
        whole.append(
            sum(ref[SP_SPEC + 48 * k : SP_SPEC + 48 * (k + 1)].astype(f32) for k in (2, 1, 0))
        )
    spec = jnp.concatenate(whole, axis=1)
    for t in range(8):
        value = jnp.zeros((ATOMS, WIDE), f32)
        for s in range(6):
            value = jnp.where(species == s, spec[8 * s + t : 8 * s + t + 1], value)
        cho_ref[t] = value


def forward_kernel(
    sc, recv, xrow, prep, rad_in, rad_t, vec, pay, geo, hid_ref, slope, hot_ref, feat_ref, acc
):
    c = sc[0]
    yh = sc[1]
    idx = prep[0:1].astype(jnp.int32)
    scaled = prep[1:2]
    rows = iota((128, EDGES), 0)
    hot = jnp.where(rows == idx, 1.0, 0.0)
    diff = (hot - jnp.where(rows == own_index(c, 0, EDGES), 1.0, 0.0)).astype(bf16)
    moved = nn(pos_table(recv, xrow, c, yh), diff)
    rel = moved[0:3] + moved[3:6] + moved[6:9]
    rx = prep[2:3] + rel[0:1]
    ry = prep[3:4] + rel[1:2]
    rz = rel[2:3]
    rho = jnp.sqrt(rx * rx + ry * ry + rz * rz + 0.25)
    inv = 1.0 / rho
    ux, uy, uz = rx * inv, ry * inv, rz * inv
    ratio = rho / cutoff
    theta = math.pi * ratio
    gap = 1.0 - ratio * ratio
    env = gap * gap * inv
    turns = (iota((8, 1), 0) + 1).astype(f32) * theta
    sins = jnp.sin(turns)
    geo[0:1] = idx.astype(f32)
    geo[1:2] = scaled
    geo[2:3] = rx
    geo[3:4] = ry
    geo[4:5] = rz
    geo[5:6] = rho
    geo[6:7] = inv
    geo[7:8] = env
    geo[8:16] = sins
    geo[16:24] = jnp.cos(turns)
    basis = sins * env
    r_hi, r_mid, r_lo = split3(rad_in[...])
    b_hi, b_mid, b_lo = split3(basis)
    z = tn(
        stacked((r_hi, r_hi, r_mid, r_hi, r_lo, r_mid)).astype(bf16),
        stacked((b_hi, b_mid, b_hi, b_lo, b_hi, b_mid)).astype(bf16),
    )
    sig = lax.logistic(z)
    hidden = (z * sig).astype(bf16)
    hid_ref[...] = hidden
    slope[...] = sig * (1.0 + z * (1.0 - sig))
    harm = (
        scaled,
        scaled * ux,
        scaled * uy,
        scaled * uz,
        scaled * ux * uy,
        scaled * uy * uz,
        scaled * (1.5 * uz * uz - 0.5),
        scaled * ux * uz,
        scaled * 0.5 * (ux * ux - uy * uy),
    )
    for m in range(9):
        geo[24 + m : 25 + m] = harm[m]
    feat_t = feat_table(recv, xrow, yh).astype(f32).T.astype(bf16)
    block = iota((PER, GROUP), 0) == (iota((PER, GROUP), 1) >> 5)
    hot_b = hot.astype(bf16)
    hot_ref[...] = hot_b
    feat_ref[...] = feat_t
    for g in range(GROUPS):
        at = slice(g * GROUP, (g + 1) * GROUP)
        nb = nn(feat_t, hot_b[:, at])
        hid = hidden[:, at]
        radials = nn(rad_t[...].reshape(3 * WIDE, HID), hid)
        for degree, (first, last) in enumerate(degree_bounds):
            p_hi, p_lo = split2(radials[degree * WIDE : (degree + 1) * WIDE] * nb)
            blocks = [jnp.where(block, harm[m][:, at], 0.0) for m in range(first, last)]
            y_hi, y_lo = split2(jnp.concatenate(blocks, axis=0))
            both = nt(jnp.concatenate([y_hi, y_lo], axis=0), p_hi)
            half = (last - first) * PER
            msg = both[:half] + both[half:] + nt(y_hi, p_lo)
            for k in range(last - first):
                r0 = (first + k) * ATOMS + g * PER
                acc[r0 : r0 + PER] = msg[k * PER : (k + 1) * PER]
    pay[0:MSG] = acc[0:MSG].astype(bf16)
    pay[MSG:PAY] = vec[...]


TOP = 14.0


def level_of(value):
    peak = jnp.max(jnp.max(jnp.abs(value), axis=0, keepdims=True), axis=1, keepdims=True)
    return jnp.clip(jnp.floor(jnp.log2(jnp.maximum(peak, 1e-30))), -100.0, 100.0)


def scale_of(adjp, s, row):
    return jnp.exp2(adjp[s, BACK + row : BACK + row + 1, 0:1] - TOP)


def mix_of(spk_o, spk_p, degree):
    at = slice(SP_MIX + 1024 * degree, SP_MIX + 1024 * (degree + 1))
    return jnp.concatenate([spk_o[at], spk_p[at]], axis=1)


def mix_kernel(sc, full, spk_o, spk_p, cho, out):
    c = sc[0]
    x = sc[2]
    at = (iota((16, WIDE), 0) * 43) >> 7
    tall = jnp.zeros((16, WIDE), f32)
    for s in range(4):
        tall = tall + full[s, MSG:PAY, :].astype(f32)
    vec = jnp.sum(jnp.where(at == x, tall, 0.0), axis=0, keepdims=True)
    vec_o, vec_p = ordered(c, vec[:, 0:CH], vec[:, CH:WIDE])
    vec = jnp.concatenate([vec_o, vec_p], axis=1)
    mixed = []
    for degree, (first, last) in enumerate(degree_bounds):
        rows = slice(first * ATOMS, last * ATOMS)
        lhs = jnp.concatenate([full[s, rows, :] for s in range(4)], axis=1)
        both = nn(lhs, mix_of(spk_o, spk_p, degree))
        for m in range(last - first):
            mixed.append(both[m * ATOMS : (m + 1) * ATOMS])

    chosen = [cho[t] for t in range(8)]
    cen, ax, ay, az, qa, qb, qc, qd, qe = mixed
    vec_sq = ax * ax + ay * ay + az * az
    quad_sq = qa * qa + qb * qb + qc * qc + qd * qd + qe * qe
    up = qe - qc
    down = qe + qc
    cubic = (
        up * ax * ax
        - down * ay * ay
        + 2.0 * qc * az * az
        + 2.0 * (qa * ax * ay + qb * ay * az + qd * ax * az)
    )
    cen_sq = cen * cen
    products = (
        cen * chosen[0]
        + cen_sq * chosen[1]
        + vec_sq * chosen[2]
        + quad_sq * chosen[3]
        + cen_sq * cen * chosen[4]
        + cen * vec_sq * chosen[5]
        + cen * quad_sq * chosen[6]
        + cubic * chosen[7]
    )
    first, second = ordered(c, products[:, 0:CH], products[:, CH:WIDE])
    prod = jnp.concatenate([first, second], axis=1).astype(bf16).astype(f32)
    w = [vec * value for value in chosen]
    a_scale = 2.0 * (w[2] + cen * w[5])
    q_scale = 2.0 * (w[3] + cen * w[6])
    w7 = w[7]
    tw7 = 2.0 * w7
    grads = [
        w[0] + 2.0 * cen * w[1] + 3.0 * cen_sq * w[4] + vec_sq * w[5] + quad_sq * w[6],
        a_scale * ax + tw7 * (up * ax + qa * ay + qd * az),
        a_scale * ay + tw7 * (qa * ax - down * ay + qb * az),
        a_scale * az + tw7 * (2.0 * qc * az + qb * ay + qd * ax),
        q_scale * qa + tw7 * ax * ay,
        q_scale * qb + tw7 * ay * az,
        q_scale * qc + w7 * (2.0 * az * az - ax * ax - ay * ay),
        q_scale * qd + tw7 * ax * az,
        q_scale * qe + w7 * (ax * ax - ay * ay),
    ]
    backs = []
    for degree, (first, last) in enumerate(degree_bounds):
        adj = jnp.concatenate(grads[first:last], axis=0).astype(bf16)
        backs.append(nt(adj, mix_of(spk_o, spk_p, degree)))
    back = jnp.concatenate(backs, axis=0)
    level_back, level_prod = level_of(back), level_of(prod)
    back = back * jnp.exp2(TOP - level_back)
    prod = prod * jnp.exp2(TOP - level_prod)
    row = iota((16, WIDE), 0)
    levels = jnp.where(row == 0, level_back, jnp.where(row == 1, level_prod, 0.0))
    for s in range(4):
        out[s, 0:MSG, :] = back[:, s * WIDE : (s + 1) * WIDE]
        out[s, MSG:BACK, :] = prod
        out[s, BACK:SENT, :] = levels


def backward_kernel(
    sc, hot, feat_t, geo, hidden, slope, rad, rad_t, rad_in, adjp, to_y, main, out
):
    c = sc[0]
    yh = sc[1]
    adjm = adjp[0, 0:MSG, :] * scale_of(adjp, 0, 0)
    for s in range(1, 4):
        adjm = adjm + adjp[s, 0:MSG, :] * scale_of(adjp, s, 0)
    r_hi, r_lo = split2(rad_in[...])
    outer = jnp.concatenate([r_hi, r_hi, r_lo], axis=1)
    order = (iota((8, 1), 0) + 1).astype(f32)
    r8 = iota((8, GROUP), 0)
    rows = iota((128, GROUP), 0)
    block = iota((PER, GROUP), 0) == (iota((PER, GROUP), 1) >> 5)

    def rows_of(x, y, z):
        return jnp.where(r8 == 0, x, jnp.where(r8 == 1, y, jnp.where(r8 == 2, z, 0.0)))

    feats = jnp.zeros((128, WIDE), f32)
    found = jnp.zeros((24, CH + 32), f32)
    for g in range(GROUPS):
        at = slice(g * GROUP, (g + 1) * GROUP)
        hot_g = hot[:, at]
        nb = nn(feat_t[...], hot_g)
        hid = hidden[:, at]
        radials = nn(rad_t[...].reshape(3 * WIDE, HID), hid)
        gh = jnp.zeros((HID, GROUP), f32)
        fb = jnp.zeros((WIDE, GROUP), f32)
        gys = []
        scaled = geo[1:2, at]
        for degree, (first, last) in enumerate(degree_bounds):
            radial = radials[degree * WIDE : (degree + 1) * WIDE]
            prod = (radial * nb).astype(bf16)
            blocks = [jnp.where(block, geo[24 + m : 25 + m, at], 0.0) for m in range(first, last)]
            y_hi, y_lo = split2(jnp.concatenate(blocks, axis=0))
            pieces = [
                adjm[m * ATOMS + g * PER : m * ATOMS + (g + 1) * PER] for m in range(first, last)
            ]
            a_hi, a_lo = split2(jnp.concatenate(pieces, axis=0))
            grad_prod = tn(
                jnp.concatenate([a_hi, a_lo, a_hi], axis=0),
                jnp.concatenate([y_hi, y_hi, y_lo], axis=0),
            )
            both = nn(jnp.concatenate([a_hi, a_lo], axis=0), prod)
            half = (last - first) * PER
            over = both[:half] + both[half:]
            for k in range(last - first):
                part = jnp.where(block, over[k * PER : (k + 1) * PER], 0.0)
                gys.append(scaled * jnp.sum(part, axis=0, keepdims=True))
            gh = gh + nn(rad[degree], (grad_prod * nb).astype(bf16))
            fb = fb + grad_prod * radial
        feats = feats + nt(hot_g, fb.astype(bf16))
        rx, ry, rz = geo[2:3, at], geo[3:4, at], geo[4:5, at]
        rho, inv, env = geo[5:6, at], geo[6:7, at], geo[7:8, at]
        d_hi, d_lo = split2(gh * slope[:, at])
        dbasis = nn(outer, jnp.concatenate([d_hi, d_lo, d_hi], axis=0))
        ratio = rho / cutoff
        gap = 1.0 - ratio * ratio
        by_cos = jnp.sum(dbasis * order * geo[16:24, at], axis=0, keepdims=True)
        by_sin = jnp.sum(dbasis * geo[8:16, at], axis=0, keepdims=True)
        drho = by_cos * (math.pi / cutoff) * env - by_sin * inv * (
            env + (4.0 / cutoff) * ratio * gap
        )
        ux, uy, uz = rx * inv, ry * inv, rz * inv
        gx_ = gys[1] + gys[4] * uy + gys[7] * uz + gys[8] * ux
        gy_ = gys[2] + gys[4] * ux + gys[5] * uz - gys[8] * uy
        gz_ = gys[3] + gys[5] * uy + 3.0 * gys[6] * uz + gys[7] * ux
        along = drho - (gx_ * ux + gy_ * uy + gz_ * uz) * inv
        eg = rows_of(gx_ * inv + ux * along, gy_ * inv + uy * along, gz_ * inv + uz * along)
        diff = jnp.where(rows == own_index(c, g * PER, GROUP), 1.0, 0.0) - hot_g.astype(f32)
        places = stacked(split3(rows_of(rx, ry, rz)) + (jnp.zeros((8, GROUP), f32),))
        against = jnp.concatenate([diff, places], axis=0).astype(bf16)
        found = found + nt(stacked(split3(eg)).astype(bf16), against)
    main[0:48] = feats[0:48]
    main[48:64] = feats[96:112]
    to_y[0:48] = feats[48:96].astype(bf16)
    to_y[48:64] = feats[112:128].astype(bf16)
    found = found[0:8] + found[8:16] + found[16:24]
    force = found[:, 0:CH]
    lane = iota((1, CH), 1)
    cross = jnp.concatenate([found[:, CH : CH + 32], jnp.zeros((8, CH - 32), f32)], axis=1)
    cross = cross + pltpu.roll(cross, CH - 8, 1) + pltpu.roll(cross, CH - 16, 1)
    virial = jnp.zeros((1, CH), f32)
    for a in range(3):
        for b in range(3):
            to = 64 + 3 * a + b
            virial = jnp.where(lane == to, pltpu.roll(cross, to - a, 1)[b : b + 1], virial)

    def placed(first, count, to):
        moved = force if to == first else pltpu.roll(force, (to - first) % CH, 1)
        return jnp.where((lane >= to) & (lane < to + count), moved, 0.0)

    def by_core(first, count, to_0, to_1):
        return jnp.where(c == 0, placed(first, count, to_0), placed(first, count, to_1))

    own, beside = sc[3], sc[4]
    goals = (
        (2 * own + yh, by_core(0, 48, 0, 16)),
        (2 * own + 1 - yh, by_core(48, 48, 0, 16)),
        (2 * beside + yh, by_core(96, 16, 48, 0)),
        (2 * beside + 1 - yh, by_core(112, 16, 48, 0)),
    )
    row = iota(out.shape, 0)
    odd = (row & 1) == 1
    total = jnp.where(odd, virial, 0.0)
    for device, value in goals:
        upper = value[0:1] + pltpu.roll(value, 64, 1)[1:2]
        chunk = jnp.where(odd, value[2:3], upper)
        total = total + jnp.where((row >> 1) == device, chunk, 0.0)
    out[...] = total


def layer_kernel(sc, recv, adjp, weights, read, layer_ref, level_ref):
    c = sc[0]
    yh = sc[1]
    parts = [adjp[s, MSG:BACK, :] * scale_of(adjp, s, 1) for s in range(4)]
    both = nn(jnp.concatenate(parts, axis=1).astype(bf16), weights[...])
    first, second = ordered(c, both[:, 0:CH], both[:, CH:WIDE])
    start = pl.multiple_of(c * 16, 16)
    own_feat = jnp.concatenate(
        [recv[2 * cs + yh, pl.ds(start, ATOMS), :].astype(f32) for cs in range(2)], axis=1
    )
    layer = jnp.concatenate([first, second], axis=1) + own_feat
    layer_ref[...] = layer.astype(bf16)
    energy = jnp.sum(layer * read[0:1], axis=1, keepdims=True)
    lane = iota((ATOMS, CH), 1)
    row = iota((ATOMS, CH), 0)
    level = jnp.sum(jnp.where(lane == row + ATOMS * c, energy, 0.0), axis=0, keepdims=True)
    level_ref[...] = jnp.broadcast_to(level, (8, CH))


def merge_kernel(sc, main, from_y, xback, layer, stay, to_core, acc):
    c = sc[0]
    acc[...] = main[0:48] + from_y[0:48].astype(f32)
    at = pl.ds(pl.multiple_of(32 * c, 16), 16)
    acc[at] = acc[at] + xback[...].astype(f32)
    feat_own, feat_other = ordered(c, acc[:, 0:CH], acc[:, CH:WIDE])
    wide = layer[...].astype(f32)
    layer_own, layer_other = ordered(c, wide[:, 0:CH], wide[:, CH:WIDE])
    stay[0:48] = feat_own.astype(bf16)
    stay[48:80] = layer_own.astype(bf16)
    to_core[0:48] = feat_other.astype(bf16)
    to_core[48:80] = layer_other.astype(bf16)


def finish_kernel(
    sc, stay, from_core, read, got, layer_out, feat_grad, energy, forces, stress, acc, *, atoms
):
    c = sc[0]
    acc[...] = jnp.broadcast_to(read[...], (64, CH))
    mine = pl.ds(pl.multiple_of(16 * c, 16), 48)
    acc[mine] = acc[mine] + stay[0:48].astype(f32)
    other = pl.ds(pl.multiple_of(16 - 16 * c, 16), 48)
    acc[other] = acc[other] + from_core[0:48].astype(f32)
    feat_grad[...] = acc[...].astype(bf16)
    layer_out[pl.ds(pl.multiple_of(ATOMS * c, ATOMS), ATOMS)] = stay[48:80]
    layer_out[pl.ds(pl.multiple_of(ATOMS - ATOMS * c, ATOMS), ATOMS)] = from_core[48:80]
    tile = got[0]
    for s in range(1, 8):
        tile = tile + got[s]
    upper, lower, level = tile[0:1], tile[1:2], tile[2:3]
    lines = (upper, pltpu.roll(upper, 64, 1), lower, level)
    row = iota((8, CH), 0)
    lane = iota((8, CH), 1)
    here = (lane < 64) & ((lane >> 4) == (row >> 1)) & ((lane & 1) == (row & 1))
    spread = jnp.concatenate([jnp.where(here, line, 0.0) for line in lines], axis=0)
    pick = jnp.where(((iota((CH, CH), 0) >> 1) & 7) == iota((CH, CH), 1), 1.0, 0.0)
    turned = lax.dot_general(
        spread, pick, (((1,), (0,)), ((), ())), precision=HIGHEST, preferred_element_type=f32
    )
    for k in range(3):
        for r in range(4):
            r0 = 8 * k + 2 * r
            forces[k, r] = turned[r0 : r0 + 2, 0:8]
    for r in range(4):
        energy[r] = turned[24 + 2 * r : 26 + 2 * r, 0:8]
    for a in range(3):
        stress[a : a + 1] = pltpu.roll(lower, CH - 64 - 3 * a, 1)[:, 0:3] * (1.0 / atoms)


def body(
    features,
    positions,
    neighbours,
    counts,
    species,
    radial_in,
    radial_out,
    mix_weight,
    species_weight,
    out_weight,
    readout,
):
    gx = lax.axis_size("g")
    every = gx * lax.axis_size("yh")
    c = lax.axis_index("core")
    own = lax.axis_index("g")
    scalars = jnp.stack(
        [c, lax.axis_index("yh"), lax.axis_index("x"), own, (own + 2 * c - 1 + gx) % gx]
    ).astype(jnp.int32)
    meta = jnp.concatenate(
        [neighbours.reshape(64, NEIGH), counts.reshape(64, 1), species.reshape(64, 1)], axis=1
    )
    shape = jax.ShapeDtypeStruct
    send = call(send_kernel, shape((4, 64, CH), bf16))(
        scalars, features.reshape(64, CH), positions.transpose(0, 1, 3, 2)
    )
    recv = lax.all_to_all(send, ("core", "yh"), 0, 0)
    radial_out, species_weight, send = lax.optimization_barrier((radial_out, species_weight, send))
    spack = call(pack_kernel, shape((SP_ROWS, CH), bf16))(
        scalars,
        radial_out.transpose(1, 0, 2).reshape(3 * HID, CH),
        species_weight.reshape(48, CH),
        readout.reshape(1, CH),
        out_weight,
        mix_weight.reshape(3 * 1024, CH),
    )
    swap = [(0, 1), (1, 0)]
    spack_p = lax.ppermute(spack, "core", swap)
    outward = [
        (co * gx + i, (1 - co) * gx + (i - 1 + 2 * co) % gx) for co in range(2) for i in range(gx)
    ]
    edge_row = call(edge_kernel, shape((4, 32, CH), bf16), us=20.0)(scalars, recv)
    xrow = lax.ppermute(edge_row, ("core", "g"), outward)
    prep, rad, rad_t, vec, cho, wide_out, wide_read = call(
        prep_kernel,
        (
            shape((8, EDGES), f32),
            shape((3, HID, WIDE), bf16),
            shape((3, WIDE, HID), bf16),
            shape((16, WIDE), bf16),
            shape((8, ATOMS, WIDE), f32),
            shape((1024, WIDE), bf16),
            shape((8, WIDE), f32),
        ),
        [pltpu.VMEM((16, WIDE), f32)],
    )(scalars, meta, spack, spack_p)
    pay, geo, hidden, slope, hot, feat_t = call(
        forward_kernel,
        (
            shape((PAY, WIDE), bf16),
            shape((40, EDGES), f32),
            shape((HID, EDGES), bf16),
            shape((HID, EDGES), f32),
            shape((128, EDGES), bf16),
            shape((WIDE, 128), bf16),
        ),
        [pltpu.VMEM((MSG, WIDE), f32)],
        us=3.2,
    )(scalars, recv, xrow, prep, radial_in, rad_t, vec)
    full = lax.all_gather(pay, "x")
    back = call(mix_kernel, shape((4, SENT, WIDE), f32), us=1.7)(
        scalars, full, spack, spack_p, cho
    )
    back = lax.optimization_barrier(back.astype(jnp.float16))
    adjp = lax.optimization_barrier(lax.all_to_all(back, "x", 0, 0)).astype(f32)
    to_y, main, leaving = call(
        backward_kernel,
        (
            shape((64, WIDE), bf16),
            shape((64, WIDE), f32),
            shape((2 * every, CH), f32),
        ),
        us=4.5,
    )(scalars, hot, feat_t, geo, hidden, slope, rad, rad_t, radial_in, adjp)
    from_y = lax.ppermute(to_y, "yh", swap)
    xsend = (main[48:64] + from_y[48:64].astype(f32)).astype(bf16)
    xback = lax.ppermute(xsend, ("core", "g"), outward)
    arrived = lax.all_to_all(leaving, ("g", "yh"), 0, 0, tiled=True)
    layer, level = call(layer_kernel, (shape((ATOMS, WIDE), bf16), shape((8, CH), f32)), us=0.5)(
        scalars, recv, adjp, wide_out, wide_read
    )
    lines = jnp.sum(arrived.reshape(every, 2, CH), axis=0)
    tile = jnp.concatenate([lines, level[0:6]], axis=0)
    small = jnp.broadcast_to(tile[None], (8, 8, CH))
    main, small = lax.optimization_barrier((main, small))
    got = lax.all_to_all(small, ("x", "core"), 0, 0)
    stay, to_core = call(
        merge_kernel,
        (shape((80, CH), bf16), shape((80, CH), bf16)),
        [pltpu.VMEM((48, WIDE), f32)],
        us=0.05,
    )(scalars, main, from_y, xback, layer)
    from_core = lax.ppermute(to_core, "core", swap)
    layer_out, feat_grad, energy, forces, stress = call(
        functools.partial(finish_kernel, atoms=64 * every),
        (
            shape((64, CH), bf16),
            shape((64, CH), bf16),
            shape((4, 2, 8), f32),
            shape((3, 4, 2, 8), f32),
            shape((3, 3), f32),
        ),
        [pltpu.VMEM((64, CH), f32)],
        us=0.05,
    )(scalars, stay, from_core, readout.reshape(1, CH), got)
    block = features.shape
    return (
        layer_out.reshape(block),
        energy.transpose(0, 2, 1),
        forces.transpose(0, 1, 3, 2),
        feat_grad.reshape(block),
        stress,
    )


def solution(mesh):
    gx = mesh.shape["gx"]
    parts = Mesh(mesh.devices.reshape(4, 2, gx, 2), ("x", "core", "g", "yh"))
    ch = ("x", "core")
    placed = (
        P("g", "yh", None, ch),
        P(None, "g", "yh", None),
        P("g", "yh", None, None),
        P("g", "yh", None),
        P("g", "yh", None),
        P(),
        P(None, None, ch),
        P(None, None, ch),
        P(None, None, ch),
        P(None, ch),
        P(ch),
    )
    return jax.shard_map(
        body,
        mesh=parts,
        in_specs=placed,
        out_specs=(
            P("g", "yh", None, ch),
            P("g", "yh", None),
            P(None, "g", "yh", None),
            P("g", "yh", None, ch),
            P(),
        ),
        check_vma=False,
    )
```

```python
import functools
import math

import jax
import jax.numpy as jnp
from jax import lax
from jax.experimental import pallas as pl
from jax.experimental.pallas import tpu as pltpu
from jax.sharding import Mesh, PartitionSpec as P

f32 = jnp.float32
bf16 = jnp.bfloat16
cutoff = 3.2
message_scale = 0.25
degree_bounds = ((0, 1), (1, 4), (4, 9))
HIGHEST = lax.Precision.HIGHEST

ATOMS = 32
NEIGH = 32
EDGES = ATOMS * NEIGH
GROUP = 1024
GROUPS = EDGES // GROUP
PER = GROUP // NEIGH
CH = 128
WIDE = 256
HID = 64
MSG = 9 * ATOMS
PAY = MSG + 16
BACK = MSG + ATOMS
SENT = BACK + 16

VMEM_LIMIT = 48 * 1024 * 1024


def nn(a, b):
    return lax.dot_general(a, b, (((1,), (0,)), ((), ())), preferred_element_type=f32)


def nt(a, b):
    return lax.dot_general(a, b, (((1,), (1,)), ((), ())), preferred_element_type=f32)


def tn(a, b):
    return lax.dot_general(a, b, (((0,), (0,)), ((), ())), preferred_element_type=f32)


def split3(v):
    hi = v.astype(bf16)
    rest = v - hi.astype(f32)
    mid = rest.astype(bf16)
    low = (rest - mid.astype(f32)).astype(bf16)
    return hi, mid, low


def split2(v):
    hi = v.astype(bf16)
    return hi, (v - hi.astype(f32)).astype(bf16)


def stacked(parts):
    return jnp.concatenate([part.astype(f32) for part in parts], axis=0)


def iota(shape, dim):
    return lax.broadcasted_iota(jnp.int32, shape, dim)


def call(kernel, out_shape, scratch=(), us=1.0):
    def run(scalars, *arrays):
        return pl.pallas_call(
            kernel,
            out_shape=out_shape,
            in_specs=[pl.BlockSpec(memory_space=pltpu.SMEM)]
            + [pl.BlockSpec(memory_space=pltpu.VMEM)] * len(arrays),
            out_specs=jax.tree.map(lambda _: pl.BlockSpec(memory_space=pltpu.VMEM), out_shape),
            scratch_shapes=list(scratch),
            cost_estimate=pl.CostEstimate(
                flops=int(us * 1e9), bytes_accessed=1 << 18, transcendentals=0
            ),
            compiler_params=pltpu.CompilerParams(vmem_limit_bytes=VMEM_LIMIT),
        )(scalars, *arrays)

    return run


SP_SPEC = 3 * HID
SP_READ = SP_SPEC + 144
SP_OUT = SP_READ + 16
SP_MIX = SP_OUT + 1024
SP_ROWS = SP_MIX + 3 * 1024


def send_kernel(sc, feat, pos, send):
    tiles = [pos[d, r] for d in range(3) for r in range(4)]
    pick = jnp.where(((iota((8, CH), 1) >> 1) & 7) == iota((8, CH), 0), 1.0, 0.0)
    spread = lax.dot_general(
        jnp.concatenate(tiles, axis=0),
        pick,
        (((1,), (0,)), ((), ())),
        precision=HIGHEST,
        preferred_element_type=f32,
    )
    r8 = iota((8, CH), 0)
    l8 = iota((8, CH), 1)
    here = (l8 < 64) & ((l8 >> 4) == (r8 >> 1)) & ((l8 & 1) == (r8 & 1))
    lines = [
        jnp.sum(jnp.where(here, spread[8 * d : 8 * d + 8], 0.0), axis=0, keepdims=True)
        for d in range(3)
    ]
    row = iota((16, CH), 0)
    rows = jnp.zeros((16, CH), f32)
    for d in range(3):
        for k, part in enumerate(split3(lines[d])):
            rows = jnp.where(row == 3 * k + d, part.astype(f32), rows)
    for c in range(2):
        moved = (rows if c == 0 else pltpu.roll(rows, CH - 16, 1)).astype(bf16)
        for y in range(2):
            send[2 * c + y, 0:48] = feat[16 * c : 16 * c + 48]
            send[2 * c + y, 48:64] = moved


def pack_kernel(sc, rad_out, spec, read, ow, mw, spack):
    spack[SP_OUT:SP_MIX] = ow[...]
    spack[SP_MIX:SP_ROWS] = mw[...]
    spack[0:SP_SPEC] = rad_out[...]
    parts = split3(spec[...])
    for k in range(3):
        spack[SP_SPEC + 48 * k : SP_SPEC + 48 * (k + 1)] = parts[k]
    r0, r1, r2 = split3(read[...])
    rr = iota((16, CH), 0)
    rows = (
        jnp.where(rr == 0, r0.astype(f32), 0.0)
        + jnp.where(rr == 1, r1.astype(f32), 0.0)
        + jnp.where(rr == 2, r2.astype(f32), 0.0)
    )
    spack[SP_READ:SP_OUT] = rows.astype(bf16)


def edge_kernel(sc, recv, out):
    start = pl.multiple_of(32 * sc[0], 16)
    for s in range(4):
        out[s, 0:16] = recv[s, pl.ds(start, 16)]
        out[s, 16:32] = recv[s, 48:64]


def feat_table(recv, xrow, yh):
    halves = []
    for cs in range(2):
        o = 2 * cs + yh
        t = 2 * cs + 1 - yh
        halves.append(
            jnp.concatenate([recv[o, 0:48], recv[t, 0:48], xrow[o, 0:16], xrow[t, 0:16]], axis=0)
        )
    return jnp.concatenate(halves, axis=1)


def pos_table(recv, xrow, c, yh):
    lane = iota((16, CH), 1)

    def turned(value, to):
        first = pltpu.roll(value, to - 32, 1)
        return jnp.where(c == 0, first, pltpu.roll(value, to, 1))

    own = recv[yh, 48:64].astype(f32)
    across = pltpu.roll(recv[1 - yh, 48:64].astype(f32), 48, 1)
    row_own = turned(xrow[yh, 16:32].astype(f32), 96)
    row_across = turned(xrow[1 - yh, 16:32].astype(f32), 112)
    table = jnp.where(
        lane < 48, own, jnp.where(lane < 96, across, jnp.where(lane < 112, row_own, row_across))
    )
    return table.astype(bf16)


def ordered(c, own, other):
    first = jnp.where(c == 0, own, other)
    second = jnp.where(c == 0, other, own)
    return first, second


def own_index(c, start, count):
    atom = (iota((1, count), 1) >> 5) + start
    return ((atom >> 4) + c) * 16 + (atom & 15)


def prep_kernel(
    sc, meta, spk_o, spk_p, rows_ref, rad_ref, rad_t_ref, vec_ref, cho_ref, ow_ref, read_ref, hot_ref, diff_ref, tmp
):
    c = sc[0]
    start = pl.multiple_of(c * ATOMS, ATOMS)
    mine = meta[pl.ds(start, ATOMS), :]
    codes = mine[:, 0:NEIGH].astype(f32).astype(bf16)
    spread = (iota((NEIGH, EDGES), 0) == (iota((NEIGH, EDGES), 1) & 31)).astype(bf16)
    at_atom = iota((ATOMS, EDGES), 0) == (iota((ATOMS, EDGES), 1) >> 5)
    code = jnp.sum(jnp.where(at_atom, nn(codes, spread), 0.0), axis=0, keepdims=True)
    code = code.astype(jnp.int32)
    counts = mine[:, NEIGH : NEIGH + 1].astype(f32)
    count = jnp.sum(jnp.where(at_atom, counts, 0.0), axis=0, keepdims=True)
    lane = iota((1, EDGES), 1)
    slot = lane & 31
    atom = lane >> 5
    col = (atom >> 1) & 7
    third = (code * 43) >> 8
    step_x = third - 1
    step_y = (code >> 1) - 3 * third - 1
    q = (atom >> 4) + step_x + c
    y = col + step_y
    across = jnp.where((y < 0) | (y > 7), 1, 0)
    inside = (q >= 0) & (q <= 2)
    idx = (
        jnp.where(inside, across * 48 + q * 16, 96 + across * 16) + (y & 7) * 2 + (code & 1)
    )
    at_row = iota((128, EDGES), 0)
    hot = jnp.where(at_row == idx, 1.0, 0.0)
    hot_ref[...] = hot.astype(bf16)
    diff_ref[...] = (jnp.where(at_row == own_index(c, 0, EDGES), 1.0, 0.0) - hot).astype(bf16)
    rows_ref[0:1] = idx.astype(f32)
    rows_ref[1:2] = jnp.where(slot.astype(f32) < count, message_scale, 0.0)
    rows_ref[2:3] = step_x.astype(f32)
    rows_ref[3:4] = step_y.astype(f32)
    rows_ref[4:8] = jnp.zeros((4, EDGES), f32)
    for degree in range(3):
        rows = slice(degree * HID, (degree + 1) * HID)
        first, second = ordered(c, spk_o[rows].astype(f32), spk_p[rows].astype(f32))
        wide = jnp.concatenate([first, second], axis=1)
        rad_ref[degree] = wide.astype(bf16)
        rad_t_ref[degree] = wide.T.astype(bf16)
    ow_ref[...] = jnp.concatenate([spk_o[SP_OUT:SP_MIX], spk_p[SP_OUT:SP_MIX]], axis=1)
    ra, rb = ordered(
        c, spk_o[SP_READ:SP_OUT].astype(f32), spk_p[SP_READ:SP_OUT].astype(f32)
    )
    read = jnp.concatenate([ra, rb], axis=1)
    read_ref[...] = jnp.broadcast_to(read[0:1] + read[1:2] + read[2:3], (8, WIDE))
    vec = 0.0
    for ref in (spk_o, spk_p):
        vec = vec + nt(ref[SP_READ:SP_OUT], ref[SP_OUT:SP_MIX])
    vec = vec[0:1] + vec[1:2] + vec[2:3]
    tmp[...] = jnp.zeros((16, WIDE), f32)
    for b in range(4):
        parts = split3(vec[:, b * WIDE : (b + 1) * WIDE])
        for k in range(3):
            tmp[3 * b + k : 3 * b + k + 1] = parts[k].astype(f32)
    vec_ref[...] = tmp[...].astype(bf16)
    species = mine[:, NEIGH + 1 : NEIGH + 2]
    whole = []
    for ref in (spk_o, spk_p):
        whole.append(
            sum(ref[SP_SPEC + 48 * k : SP_SPEC + 48 * (k + 1)].astype(f32) for k in (2, 1, 0))
        )
    spec = jnp.concatenate(whole, axis=1)
    for t in range(8):
        value = jnp.zeros((ATOMS, WIDE), f32)
        for s in range(6):
            value = jnp.where(species == s, spec[8 * s + t : 8 * s + t + 1], value)
        cho_ref[t] = value


def forward_kernel(
    sc, recv, xrow, prep, hot, diff, rad_in, rad_t, vec, pay, geo, hid_ref, slope, feat_ref, acc
):
    c = sc[0]
    yh = sc[1]
    scaled = prep[1:2]
    moved = -nn(pos_table(recv, xrow, c, yh), diff[...])
    rel = moved[0:3] + moved[3:6] + moved[6:9]
    rx = prep[2:3] + rel[0:1]
    ry = prep[3:4] + rel[1:2]
    rz = rel[2:3]
    rho = jnp.sqrt(rx * rx + ry * ry + rz * rz + 0.25)
    inv = 1.0 / rho
    ux, uy, uz = rx * inv, ry * inv, rz * inv
    ratio = rho / cutoff
    theta = math.pi * ratio
    gap = 1.0 - ratio * ratio
    env = gap * gap * inv
    turns = (iota((8, 1), 0) + 1).astype(f32) * theta
    sins = jnp.sin(turns)
    geo[0:1] = scaled
    geo[1:2] = scaled
    geo[2:3] = rx
    geo[3:4] = ry
    geo[4:5] = rz
    geo[5:6] = rho
    geo[6:7] = inv
    geo[7:8] = env
    geo[8:16] = sins
    geo[16:24] = jnp.cos(turns)
    basis = sins * env
    r_hi, r_mid, r_lo = split3(rad_in[...])
    b_hi, b_mid, b_lo = split3(basis)
    z = tn(
        stacked((r_hi, r_hi, r_mid, r_hi, r_lo, r_mid)).astype(bf16),
        stacked((b_hi, b_mid, b_hi, b_lo, b_hi, b_mid)).astype(bf16),
    )
    sig = lax.logistic(z)
    hidden = (z * sig).astype(bf16)
    hid_ref[...] = hidden
    slope[...] = sig * (1.0 + z * (1.0 - sig))
    harm = (
        scaled,
        scaled * ux,
        scaled * uy,
        scaled * uz,
        scaled * ux * uy,
        scaled * uy * uz,
        scaled * (1.5 * uz * uz - 0.5),
        scaled * ux * uz,
        scaled * 0.5 * (ux * ux - uy * uy),
    )
    for m in range(9):
        geo[24 + m : 25 + m] = harm[m]
    feat_t = feat_table(recv, xrow, yh).astype(f32).T.astype(bf16)
    block = iota((PER, GROUP), 0) == (iota((PER, GROUP), 1) >> 5)
    feat_ref[...] = feat_t
    for g in range(GROUPS):
        at = slice(g * GROUP, (g + 1) * GROUP)
        nb = nn(feat_t, hot[:, at])
        hid = hidden[:, at]
        radials = nn(rad_t[...].reshape(3 * WIDE, HID), hid)
        for degree, (first, last) in enumerate(degree_bounds):
            p_hi, p_lo = split2(radials[degree * WIDE : (degree + 1) * WIDE] * nb)
            blocks = [jnp.where(block, harm[m][:, at], 0.0) for m in range(first, last)]
            y_hi, y_lo = split2(jnp.concatenate(blocks, axis=0))
            both = nt(jnp.concatenate([y_hi, y_lo], axis=0), p_hi)
            half = (last - first) * PER
            msg = both[:half] + both[half:] + nt(y_hi, p_lo)
            for k in range(last - first):
                r0 = (first + k) * ATOMS + g * PER
                acc[r0 : r0 + PER] = msg[k * PER : (k + 1) * PER]
    message = acc[0:MSG].astype(bf16)
    for s in range(4):
        pay[s, 0:MSG] = message
        pay[s, MSG:PAY] = vec[...]


TOP = 14.0


def level_of(value):
    peak = jnp.max(jnp.max(jnp.abs(value), axis=0, keepdims=True), axis=1, keepdims=True)
    return jnp.clip(jnp.floor(jnp.log2(jnp.maximum(peak, 1e-30))), -100.0, 100.0)


def scale_of(adjp, s, row):
    return jnp.exp2(adjp[s, BACK + row : BACK + row + 1, 0:1] - TOP)


def mix_of(spk_o, spk_p, degree):
    at = slice(SP_MIX + 1024 * degree, SP_MIX + 1024 * (degree + 1))
    return jnp.concatenate([spk_o[at], spk_p[at]], axis=1)


def mix_kernel(sc, full, spk_o, spk_p, cho, out):
    c = sc[0]
    x = sc[2]
    at = (iota((16, WIDE), 0) * 43) >> 7
    tall = jnp.zeros((16, WIDE), f32)
    for s in range(4):
        tall = tall + full[s, MSG:PAY, :].astype(f32)
    vec = jnp.sum(jnp.where(at == x, tall, 0.0), axis=0, keepdims=True)
    vec_o, vec_p = ordered(c, vec[:, 0:CH], vec[:, CH:WIDE])
    vec = jnp.concatenate([vec_o, vec_p], axis=1)
    mixed = []
    for degree, (first, last) in enumerate(degree_bounds):
        rows = slice(first * ATOMS, last * ATOMS)
        lhs = jnp.concatenate([full[s, rows, :] for s in range(4)], axis=1)
        both = nn(lhs, mix_of(spk_o, spk_p, degree))
        for m in range(last - first):
            mixed.append(both[m * ATOMS : (m + 1) * ATOMS])

    chosen = [cho[t] for t in range(8)]
    cen, ax, ay, az, qa, qb, qc, qd, qe = mixed
    vec_sq = ax * ax + ay * ay + az * az
    quad_sq = qa * qa + qb * qb + qc * qc + qd * qd + qe * qe
    up = qe - qc
    down = qe + qc
    cubic = (
        up * ax * ax
        - down * ay * ay
        + 2.0 * qc * az * az
        + 2.0 * (qa * ax * ay + qb * ay * az + qd * ax * az)
    )
    cen_sq = cen * cen
    products = (
        cen * chosen[0]
        + cen_sq * chosen[1]
        + vec_sq * chosen[2]
        + quad_sq * chosen[3]
        + cen_sq * cen * chosen[4]
        + cen * vec_sq * chosen[5]
        + cen * quad_sq * chosen[6]
        + cubic * chosen[7]
    )
    first, second = ordered(c, products[:, 0:CH], products[:, CH:WIDE])
    prod = jnp.concatenate([first, second], axis=1).astype(bf16).astype(f32)
    w = [vec * value for value in chosen]
    a_scale = 2.0 * (w[2] + cen * w[5])
    q_scale = 2.0 * (w[3] + cen * w[6])
    w7 = w[7]
    tw7 = 2.0 * w7
    grads = [
        w[0] + 2.0 * cen * w[1] + 3.0 * cen_sq * w[4] + vec_sq * w[5] + quad_sq * w[6],
        a_scale * ax + tw7 * (up * ax + qa * ay + qd * az),
        a_scale * ay + tw7 * (qa * ax - down * ay + qb * az),
        a_scale * az + tw7 * (2.0 * qc * az + qb * ay + qd * ax),
        q_scale * qa + tw7 * ax * ay,
        q_scale * qb + tw7 * ay * az,
        q_scale * qc + w7 * (2.0 * az * az - ax * ax - ay * ay),
        q_scale * qd + tw7 * ax * az,
        q_scale * qe + w7 * (ax * ax - ay * ay),
    ]
    backs = []
    for degree, (first, last) in enumerate(degree_bounds):
        adj = jnp.concatenate(grads[first:last], axis=0).astype(bf16)
        backs.append(nt(adj, mix_of(spk_o, spk_p, degree)))
    back = jnp.concatenate(backs, axis=0)
    level_back, level_prod = level_of(back), level_of(prod)
    back = back * jnp.exp2(TOP - level_back)
    prod = prod * jnp.exp2(TOP - level_prod)
    row = iota((16, WIDE), 0)
    levels = jnp.where(row == 0, level_back, jnp.where(row == 1, level_prod, 0.0))
    for s in range(4):
        out[s, 0:MSG, :] = back[:, s * WIDE : (s + 1) * WIDE]
        out[s, MSG:BACK, :] = prod
        out[s, BACK:SENT, :] = levels


def backward_kernel(
    sc, hot, diff, feat_t, geo, hidden, slope, rad, rad_t, rad_in, adjp, to_y, main, out
):
    c = sc[0]
    yh = sc[1]
    adjm = adjp[0, 0:MSG, :] * scale_of(adjp, 0, 0)
    for s in range(1, 4):
        adjm = adjm + adjp[s, 0:MSG, :] * scale_of(adjp, s, 0)
    r_hi, r_lo = split2(rad_in[...])
    outer = jnp.concatenate([r_hi, r_hi, r_lo], axis=1)
    order = (iota((8, 1), 0) + 1).astype(f32)
    r8 = iota((8, GROUP), 0)
    block = iota((PER, GROUP), 0) == (iota((PER, GROUP), 1) >> 5)

    def rows_of(x, y, z):
        return jnp.where(r8 == 0, x, jnp.where(r8 == 1, y, jnp.where(r8 == 2, z, 0.0)))

    feats = jnp.zeros((128, WIDE), f32)
    found = jnp.zeros((24, CH + 32), f32)
    for g in range(GROUPS):
        at = slice(g * GROUP, (g + 1) * GROUP)
        hot_g = hot[:, at]
        nb = nn(feat_t[...], hot_g)
        hid = hidden[:, at]
        radials = nn(rad_t[...].reshape(3 * WIDE, HID), hid)
        gh = jnp.zeros((HID, GROUP), f32)
        fb = jnp.zeros((WIDE, GROUP), f32)
        gys = []
        scaled = geo[1:2, at]
        for degree, (first, last) in enumerate(degree_bounds):
            radial = radials[degree * WIDE : (degree + 1) * WIDE]
            prod = (radial * nb).astype(bf16)
            blocks = [jnp.where(block, geo[24 + m : 25 + m, at], 0.0) for m in range(first, last)]
            y_hi, y_lo = split2(jnp.concatenate(blocks, axis=0))
            pieces = [
                adjm[m * ATOMS + g * PER : m * ATOMS + (g + 1) * PER] for m in range(first, last)
            ]
            a_hi, a_lo = split2(jnp.concatenate(pieces, axis=0))
            grad_prod = tn(
                jnp.concatenate([a_hi, a_lo, a_hi], axis=0),
                jnp.concatenate([y_hi, y_hi, y_lo], axis=0),
            )
            both = nn(jnp.concatenate([a_hi, a_lo], axis=0), prod)
            half = (last - first) * PER
            over = both[:half] + both[half:]
            for k in range(last - first):
                part = jnp.where(block, over[k * PER : (k + 1) * PER], 0.0)
                gys.append(scaled * jnp.sum(part, axis=0, keepdims=True))
            gh = gh + nn(rad[degree], (grad_prod * nb).astype(bf16))
            fb = fb + grad_prod * radial
        feats = feats + nt(hot_g, fb.astype(bf16))
        rx, ry, rz = geo[2:3, at], geo[3:4, at], geo[4:5, at]
        rho, inv, env = geo[5:6, at], geo[6:7, at], geo[7:8, at]
        d_hi, d_lo = split2(gh * slope[:, at])
        dbasis = nn(outer, jnp.concatenate([d_hi, d_lo, d_hi], axis=0))
        ratio = rho / cutoff
        gap = 1.0 - ratio * ratio
        by_cos = jnp.sum(dbasis * order * geo[16:24, at], axis=0, keepdims=True)
        by_sin = jnp.sum(dbasis * geo[8:16, at], axis=0, keepdims=True)
        drho = by_cos * (math.pi / cutoff) * env - by_sin * inv * (
            env + (4.0 / cutoff) * ratio * gap
        )
        ux, uy, uz = rx * inv, ry * inv, rz * inv
        gx_ = gys[1] + gys[4] * uy + gys[7] * uz + gys[8] * ux
        gy_ = gys[2] + gys[4] * ux + gys[5] * uz - gys[8] * uy
        gz_ = gys[3] + gys[5] * uy + 3.0 * gys[6] * uz + gys[7] * ux
        along = drho - (gx_ * ux + gy_ * uy + gz_ * uz) * inv
        eg = rows_of(gx_ * inv + ux * along, gy_ * inv + uy * along, gz_ * inv + uz * along)
        places = stacked(split3(rows_of(rx, ry, rz)) + (jnp.zeros((8, GROUP), f32),))
        against = jnp.concatenate([diff[:, at], places.astype(bf16)], axis=0)
        found = found + nt(stacked(split3(eg)).astype(bf16), against)
    main[0:48] = feats[0:48]
    main[48:64] = feats[96:112]
    to_y[0:48] = feats[48:96].astype(bf16)
    to_y[48:64] = feats[112:128].astype(bf16)
    found = found[0:8] + found[8:16] + found[16:24]
    force = found[:, 0:CH]
    lane = iota((1, CH), 1)
    cross = jnp.concatenate([found[:, CH : CH + 32], jnp.zeros((8, CH - 32), f32)], axis=1)
    cross = cross + pltpu.roll(cross, CH - 8, 1) + pltpu.roll(cross, CH - 16, 1)
    virial = jnp.zeros((1, CH), f32)
    for a in range(3):
        for b in range(3):
            to = 64 + 3 * a + b
            virial = jnp.where(lane == to, pltpu.roll(cross, to - a, 1)[b : b + 1], virial)

    def placed(first, count, to):
        moved = force if to == first else pltpu.roll(force, (to - first) % CH, 1)
        return jnp.where((lane >= to) & (lane < to + count), moved, 0.0)

    def by_core(first, count, to_0, to_1):
        return jnp.where(c == 0, placed(first, count, to_0), placed(first, count, to_1))

    own, beside = sc[3], sc[4]
    goals = (
        (2 * own + yh, by_core(0, 48, 0, 16)),
        (2 * own + 1 - yh, by_core(48, 48, 0, 16)),
        (2 * beside + yh, by_core(96, 16, 48, 0)),
        (2 * beside + 1 - yh, by_core(112, 16, 48, 0)),
    )
    row = iota(out.shape, 0)
    odd = (row & 1) == 1
    total = jnp.where(odd, virial, 0.0)
    for device, value in goals:
        upper = value[0:1] + pltpu.roll(value, 64, 1)[1:2]
        chunk = jnp.where(odd, value[2:3], upper)
        total = total + jnp.where((row >> 1) == device, chunk, 0.0)
    out[...] = total


def layer_kernel(sc, recv, adjp, weights, read, layer_ref, level_ref):
    c = sc[0]
    yh = sc[1]
    parts = [adjp[s, MSG:BACK, :] * scale_of(adjp, s, 1) for s in range(4)]
    both = nn(jnp.concatenate(parts, axis=1).astype(bf16), weights[...])
    first, second = ordered(c, both[:, 0:CH], both[:, CH:WIDE])
    start = pl.multiple_of(c * 16, 16)
    own_feat = jnp.concatenate(
        [recv[2 * cs + yh, pl.ds(start, ATOMS), :].astype(f32) for cs in range(2)], axis=1
    )
    layer = jnp.concatenate([first, second], axis=1) + own_feat
    layer_ref[...] = layer.astype(bf16)
    energy = jnp.sum(layer * read[0:1], axis=1, keepdims=True)
    lane = iota((ATOMS, CH), 1)
    row = iota((ATOMS, CH), 0)
    level = jnp.sum(jnp.where(lane == row + ATOMS * c, energy, 0.0), axis=0, keepdims=True)
    level_ref[...] = jnp.broadcast_to(level, (8, CH))


def merge_kernel(sc, main, from_y, xback, layer, stay, to_core, acc):
    c = sc[0]
    acc[...] = main[0:48] + from_y[0:48].astype(f32)
    at = pl.ds(pl.multiple_of(32 * c, 16), 16)
    acc[at] = acc[at] + xback[...].astype(f32)
    feat_own, feat_other = ordered(c, acc[:, 0:CH], acc[:, CH:WIDE])
    wide = layer[...].astype(f32)
    layer_own, layer_other = ordered(c, wide[:, 0:CH], wide[:, CH:WIDE])
    stay[0:48] = feat_own.astype(bf16)
    stay[48:80] = layer_own.astype(bf16)
    to_core[0:48] = feat_other.astype(bf16)
    to_core[48:80] = layer_other.astype(bf16)


def finish_kernel(
    sc, stay, from_core, read, got, layer_out, feat_grad, energy, forces, stress, acc, *, atoms
):
    c = sc[0]
    acc[...] = jnp.broadcast_to(read[...], (64, CH))
    mine = pl.ds(pl.multiple_of(16 * c, 16), 48)
    acc[mine] = acc[mine] + stay[0:48].astype(f32)
    other = pl.ds(pl.multiple_of(16 - 16 * c, 16), 48)
    acc[other] = acc[other] + from_core[0:48].astype(f32)
    feat_grad[...] = acc[...].astype(bf16)
    layer_out[pl.ds(pl.multiple_of(ATOMS * c, ATOMS), ATOMS)] = stay[48:80]
    layer_out[pl.ds(pl.multiple_of(ATOMS - ATOMS * c, ATOMS), ATOMS)] = from_core[48:80]
    tile = got[0]
    for s in range(1, 8):
        tile = tile + got[s]
    upper, lower, level = tile[0:1], tile[1:2], tile[2:3]
    lines = (upper, pltpu.roll(upper, 64, 1), lower, level)
    row = iota((8, CH), 0)
    lane = iota((8, CH), 1)
    here = (lane < 64) & ((lane >> 4) == (row >> 1)) & ((lane & 1) == (row & 1))
    spread = jnp.concatenate([jnp.where(here, line, 0.0) for line in lines], axis=0)
    pick = jnp.where(((iota((CH, CH), 0) >> 1) & 7) == iota((CH, CH), 1), 1.0, 0.0)
    turned = lax.dot_general(
        spread, pick, (((1,), (0,)), ((), ())), precision=HIGHEST, preferred_element_type=f32
    )
    for k in range(3):
        for r in range(4):
            r0 = 8 * k + 2 * r
            forces[k, r] = turned[r0 : r0 + 2, 0:8]
    for r in range(4):
        energy[r] = turned[24 + 2 * r : 26 + 2 * r, 0:8]
    for a in range(3):
        stress[a : a + 1] = pltpu.roll(lower, CH - 64 - 3 * a, 1)[:, 0:3] * (1.0 / atoms)


def body(
    features,
    positions,
    neighbours,
    counts,
    species,
    radial_in,
    radial_out,
    mix_weight,
    species_weight,
    out_weight,
    readout,
):
    gx = lax.axis_size("g")
    every = gx * lax.axis_size("yh")
    c = lax.axis_index("core")
    own = lax.axis_index("g")
    scalars = jnp.stack(
        [c, lax.axis_index("yh"), lax.axis_index("x"), own, (own + 2 * c - 1 + gx) % gx]
    ).astype(jnp.int32)
    meta = jnp.concatenate(
        [neighbours.reshape(64, NEIGH), counts.reshape(64, 1), species.reshape(64, 1)], axis=1
    )
    shape = jax.ShapeDtypeStruct
    send = call(send_kernel, shape((4, 64, CH), bf16))(
        scalars, features.reshape(64, CH), positions.transpose(0, 1, 3, 2)
    )
    recv = lax.all_to_all(send, ("core", "yh"), 0, 0)
    radial_out, species_weight, send = lax.optimization_barrier((radial_out, species_weight, send))
    spack = call(pack_kernel, shape((SP_ROWS, CH), bf16))(
        scalars,
        radial_out.transpose(1, 0, 2).reshape(3 * HID, CH),
        species_weight.reshape(48, CH),
        readout.reshape(1, CH),
        out_weight,
        mix_weight.reshape(3 * 1024, CH),
    )
    swap = [(0, 1), (1, 0)]
    spack_p = lax.ppermute(spack, "core", swap)
    outward = [
        (co * gx + i, (1 - co) * gx + (i - 1 + 2 * co) % gx) for co in range(2) for i in range(gx)
    ]
    edge_row = call(edge_kernel, shape((4, 32, CH), bf16), us=20.0)(scalars, recv)
    xrow = lax.ppermute(edge_row, ("core", "g"), outward)
    prep, rad, rad_t, vec, cho, wide_out, wide_read, hot, diff = call(
        prep_kernel,
        (
            shape((8, EDGES), f32),
            shape((3, HID, WIDE), bf16),
            shape((3, WIDE, HID), bf16),
            shape((16, WIDE), bf16),
            shape((8, ATOMS, WIDE), f32),
            shape((1024, WIDE), bf16),
            shape((8, WIDE), f32),
            shape((128, EDGES), bf16),
            shape((128, EDGES), bf16),
        ),
        [pltpu.VMEM((16, WIDE), f32)],
    )(scalars, meta, spack, spack_p)
    pay, geo, hidden, slope, feat_t = call(
        forward_kernel,
        (
            shape((4, PAY, WIDE), bf16),
            shape((40, EDGES), f32),
            shape((HID, EDGES), bf16),
            shape((HID, EDGES), f32),
            shape((WIDE, 128), bf16),
        ),
        [pltpu.VMEM((MSG, WIDE), f32)],
        us=3.2,
    )(scalars, recv, xrow, prep, hot, diff, radial_in, rad_t, vec)
    full = lax.all_to_all(pay, "x", 0, 0)
    back = call(mix_kernel, shape((4, SENT, WIDE), f32), us=1.7)(
        scalars, full, spack, spack_p, cho
    )
    back = lax.optimization_barrier(back.astype(jnp.float16))
    adjp = lax.optimization_barrier(lax.all_to_all(back, "x", 0, 0)).astype(f32)
    to_y, main, leaving = call(
        backward_kernel,
        (
            shape((64, WIDE), bf16),
            shape((64, WIDE), f32),
            shape((2 * every, CH), f32),
        ),
        us=4.5,
    )(scalars, hot, diff, feat_t, geo, hidden, slope, rad, rad_t, radial_in, adjp)
    from_y = lax.ppermute(to_y, "yh", swap)
    xsend = (main[48:64] + from_y[48:64].astype(f32)).astype(bf16)
    xback = lax.ppermute(xsend, ("core", "g"), outward)
    arrived = lax.all_to_all(leaving, ("g", "yh"), 0, 0, tiled=True)
    layer, level = call(layer_kernel, (shape((ATOMS, WIDE), bf16), shape((8, CH), f32)), us=0.5)(
        scalars, recv, adjp, wide_out, wide_read
    )
    lines = jnp.sum(arrived.reshape(every, 2, CH), axis=0)
    tile = jnp.concatenate([lines, level[0:6]], axis=0)
    small = jnp.broadcast_to(tile[None], (8, 8, CH))
    main, small = lax.optimization_barrier((main, small))
    got = lax.all_to_all(small, ("x", "core"), 0, 0)
    stay, to_core = call(
        merge_kernel,
        (shape((80, CH), bf16), shape((80, CH), bf16)),
        [pltpu.VMEM((48, WIDE), f32)],
        us=0.05,
    )(scalars, main, from_y, xback, layer)
    from_core = lax.ppermute(to_core, "core", swap)
    layer_out, feat_grad, energy, forces, stress = call(
        functools.partial(finish_kernel, atoms=64 * every),
        (
            shape((64, CH), bf16),
            shape((64, CH), bf16),
            shape((4, 2, 8), f32),
            shape((3, 4, 2, 8), f32),
            shape((3, 3), f32),
        ),
        [pltpu.VMEM((64, CH), f32)],
        us=0.05,
    )(scalars, stay, from_core, readout.reshape(1, CH), got)
    block = features.shape
    return (
        layer_out.reshape(block),
        energy.transpose(0, 2, 1),
        forces.transpose(0, 1, 3, 2),
        feat_grad.reshape(block),
        stress,
    )


def solution(mesh):
    gx = mesh.shape["gx"]
    parts = Mesh(mesh.devices.reshape(4, 2, gx, 2), ("x", "core", "g", "yh"))
    ch = ("x", "core")
    placed = (
        P("g", "yh", None, ch),
        P(None, "g", "yh", None),
        P("g", "yh", None, None),
        P("g", "yh", None),
        P("g", "yh", None),
        P(),
        P(None, None, ch),
        P(None, None, ch),
        P(None, None, ch),
        P(None, ch),
        P(ch),
    )
    return jax.shard_map(
        body,
        mesh=parts,
        in_specs=placed,
        out_specs=(
            P("g", "yh", None, ch),
            P("g", "yh", None),
            P(None, "g", "yh", None),
            P("g", "yh", None, ch),
            P(),
        ),
        check_vma=False,
    )
```
